128 devices in a mesh: dp: 32 (over y, x, core), vis: 4 (over z).
Axes of the slice: x: 4, y: 4, z: 4, core: 2. Of those that a mesh axis runs over, the one named last changes fastest.
Arguments:
- patches: bfloat16 [65536, 1280], P(('dp', 'vis')), may hold values from -100 to 100
- window_index: int32 [128, 512], P(('dp', 'vis')), may hold values from 0 to 511, each once within a row
- window_live: int32 [128, 8], P(('dp', 'vis')), may hold values from 0 to 64, as said below
- d_merged: bfloat16 [16384, 5120], P(('dp', 'vis')), may hold values from -1 to 1
- w_qkv: bfloat16 [1280, 2880], replicated, may hold values from -20 to 20
- w_out: bfloat16 [960, 1280], replicated, may hold values from -0.1875 to 0.1875
- merge_gain: float32 [1280], replicated, may hold values from 0.1 to 1.9
Outputs:
- merged: bfloat16 [16384, 5120], P(('dp', 'vis'))
- grad_qkv: float32 [1280, 2880], P(('dp', 'vis'))
- grad_out: float32 [960, 1280], P(None, ('dp', 'vis'))
- grad_gain: float32 [1280], P(('dp', 'vis'))
The draws below stay inside these ranges and needn't reach their ends.
Inputs may be any that keep to these rules, and one draw needn't show every extreme that they name: `window_live`: entry [i, w] gives the live rows of window slot w of device i = dp * 4 + vis: 0 for an empty slot, else a multiple of 4. On every device the slots with live rows come first. In every vis column the 32 owners hold together exactly 128 windows with live rows.
All inputs are finite; a program needn't handle non-finite values.
Results may differ from the reference program's by a relative error of at most 0.018.
Values may be sent and summed in bfloat16 or wider, within the bound.
A program may use at most 192 MiB of HBM per device.

```python
import math
import jax
import jax.numpy as jnp
from jax import lax

D = 1280
HEADS = 12
HEAD_DIM = 80
WIN = 64
W_DEV = 8
N_DP = 32
N_VIS = 4


def draw_patches(key, part):
    key = jax.random.fold_in(key, 11)
    first_key, second_key, third_key = jax.random.split(key, 3)
    total_rows = N_DP * N_VIS * W_DEV * WIN
    row_scale = 0.3 * jnp.exp(jax.random.uniform(second_key, (total_rows, 1), jnp.float32, 0.0, math.log(10.0)))
    col_scale = 0.3 * jnp.exp(jax.random.uniform(third_key, (1, D), jnp.float32, 0.0, math.log(10.0)))
    base = jnp.clip(jax.random.normal(first_key, (total_rows, D), jnp.float32), -6.0, 6.0)
    return (base * row_scale * 3.0 * col_scale * 3.0 * 0.1).astype(jnp.bfloat16)


def draw_d_merged(key, part):
    key = jax.random.fold_in(key, 17)
    total_rows = N_DP * N_VIS * W_DEV * WIN
    shape_out = (total_rows // 4, 4 * D)
    factor = total_rows ** (-0.5)
    base = jnp.clip(jax.random.normal(key, shape_out, jnp.float32), -6.0, 6.0)
    return (base * factor).astype(jnp.bfloat16)


def draw_w_qkv(key, part):
    key = jax.random.fold_in(key, 23)
    first_key = jax.random.fold_in(key, 0)
    inner_width = HEADS * HEAD_DIM
    full = jnp.clip(jax.random.normal(first_key, (D, 3 * inner_width), jnp.float32), -6.0, 6.0) * D ** (-0.5)
    return full.astype(jnp.bfloat16)


def draw_window_live(key, part):
    key = jax.random.fold_in(key, 5)
    keys_all = jax.random.split(key, 4)
    half_ranks = N_DP // 2
    split_at = jax.random.randint(keys_all[0], (N_VIS, half_ranks), 0, W_DEV + 1)
    split_at = split_at.at[:, 0].set(W_DEV)
    counts = jnp.concatenate([split_at, W_DEV - split_at], axis=1)
    orders = jax.vmap(lambda one_key: jax.random.permutation(one_key, N_DP))(jax.random.split(keys_all[1], N_VIS))
    counts = jnp.take_along_axis(counts, orders, axis=1)
    fully = jax.random.randint(keys_all[2], (N_VIS, N_DP, W_DEV), 0, 4) > 0
    partly = 4 * jax.random.randint(keys_all[3], (N_VIS, N_DP, W_DEV), 1, WIN // 4)
    live_rows = jnp.where(fully, WIN, partly)
    slot_ids = jnp.arange(W_DEV, dtype=jnp.int32)
    live_rows = jnp.where(slot_ids[None, None, :] < counts[:, :, None], live_rows, 0)
    forced = (counts[:, :, None] == W_DEV) & (slot_ids[None, None, :] == 0)
    live_rows = jnp.where(forced, WIN, live_rows)
    return jnp.transpose(live_rows, (1, 0, 2)).reshape(N_DP * N_VIS, W_DEV).astype(jnp.int32)


def bell_draw(stream_key, dims, spread, most, kind=jnp.bfloat16):
    drawn = jax.random.normal(stream_key, dims, jnp.float32) * spread
    return jnp.minimum(jnp.maximum(drawn, -most), most).astype(kind)


def setup_inputs(seed: int = 0) -> dict:
    streams_of = jax.random.split(jax.random.key(seed), 8)
    return {
        "patches": draw_patches(jax.random.fold_in(streams_of[7], 71), 0),
        "window_index": jax.vmap(lambda own: jax.random.permutation(own, W_DEV * WIN))(jax.random.split(streams_of[1], (N_DP * N_VIS))).reshape((N_DP * N_VIS, W_DEV * WIN)).astype(jnp.int32),
        "window_live": draw_window_live(jax.random.fold_in(streams_of[7], 71), 0),
        "d_merged": draw_d_merged(jax.random.fold_in(streams_of[7], 71), 0),
        "w_qkv": draw_w_qkv(jax.random.fold_in(streams_of[7], 71), 0),
        "w_out": bell_draw(streams_of[5], (HEADS * HEAD_DIM, D), (HEADS * HEAD_DIM) ** -0.5, 0.1875),
        "merge_gain": jnp.clip(1.0 + 0.18 * jax.random.normal(streams_of[6], (D,), jnp.float32), 0.1, 1.9),
    }


EPSILON = 1e-06
NEGATIVE = -1e+30

def contract(formula, first_op, second_op):
    return jnp.einsum(formula, first_op.astype(jnp.float32), second_op.astype(jnp.float32))

def lower(values_in):
    return lax.optimization_barrier(values_in.astype(jnp.bfloat16))

def forward(window_rows, live_rows, w_qkv, w_out, merge_gain):
    window_count, win_rows, model_width = window_rows.shape
    inner_width = w_out.shape[0]
    head_width = inner_width // HEADS
    widened = window_rows.astype(jnp.float32)
    normed = lower(widened * lax.rsqrt(lax.optimization_barrier(jnp.mean(widened * widened, -1, keepdims=True)) + EPSILON))
    packed = lower(contract('bwd,de->bwe', normed, w_qkv))
    packed = packed.reshape(window_count, win_rows, 3, HEADS, head_width)
    query = packed[:, :, 0]
    key_rows = packed[:, :, 1]
    values = packed[:, :, 2]
    scores = contract('bqhc,bkhc->bhqk', query, key_rows) * head_width ** (-0.5)
    alive = jnp.arange(win_rows)[None, :] < live_rows[:, None]
    scores = jnp.where(alive[:, None, None, :], scores, NEGATIVE)
    probs = jax.nn.softmax(scores, axis=-1)
    probs_low = lower(probs)
    context = lower(contract('bhqk,bkhc->bqhc', probs_low, values)).reshape(window_count, win_rows, inner_width)
    attended = widened + contract('bwi,id->bwd', context, w_out)
    inverse = lax.rsqrt(lax.optimization_barrier(jnp.mean(attended * attended, -1, keepdims=True)) + EPSILON)
    normalized = attended * inverse
    row_mask = alive[:, :, None].astype(jnp.float32)
    merged = (normalized * merge_gain * row_mask).astype(jnp.bfloat16).reshape(window_count, win_rows // 4, 4 * model_width)
    saved = (normed, query, key_rows, values, probs, probs_low, context, normalized, inverse, row_mask)
    return (merged, saved)

def backward(saved, cotangent, w_out, merge_gain):
    normed, query, key_rows, values, probs, probs_low, context, normalized, inverse, row_mask = saved
    window_count, win_rows, model_width = normalized.shape
    head_width = query.shape[-1]
    grad_rows = cotangent.astype(jnp.float32).reshape(window_count, win_rows, model_width) * row_mask
    grad_gain = lax.optimization_barrier(jnp.sum(grad_rows * normalized, axis=(0, 1)))
    scaled = grad_rows * merge_gain
    d_attended = lower(inverse * (scaled - normalized * lax.optimization_barrier(jnp.mean(scaled * normalized, -1, keepdims=True))))
    grad_out = contract('bwi,bwd->id', context, d_attended)
    d_context = lower(contract('bwd,id->bwi', d_attended, w_out)).reshape(window_count, win_rows, HEADS, head_width)
    d_values = contract('bhqk,bqhc->bkhc', probs_low, d_context)
    d_probs = contract('bqhc,bkhc->bhqk', d_context, values)
    d_scores = lower(probs * (d_probs - lax.optimization_barrier(jnp.sum(d_probs * probs, -1, keepdims=True))) * head_width ** (-0.5))
    d_query = contract('bhqk,bkhc->bqhc', d_scores, key_rows)
    d_keys = contract('bhqk,bqhc->bkhc', d_scores, query)
    d_packed = lower(jnp.stack([d_query, d_keys, d_values], axis=2)).reshape(window_count, win_rows, -1)
    grad_qkv = contract('bwd,bwe->de', normed, d_packed)
    return (grad_qkv, grad_out, grad_gain)

def reference(patches, window_index, window_live, d_merged, w_qkv, w_out, merge_gain):
    device_count = N_DP * N_VIS
    block_rows = patches.reshape(device_count, W_DEV * WIN, D)
    cot_blocks = d_merged.reshape(device_count, W_DEV, WIN // 4, 4 * D)
    inner_width = HEADS * HEAD_DIM

    def step(carry, pieces):
        block, order, live_rows, cot_block = pieces
        window_rows = jnp.take(block, order.astype(jnp.int32), axis=0).reshape(W_DEV, WIN, D)
        merged, saved = forward(window_rows, live_rows, w_qkv, w_out, merge_gain)
        grad_qkv, grad_out, grad_gain = backward(saved, cot_block, w_out, merge_gain)
        return ((carry[0] + grad_qkv, carry[1] + grad_out, carry[2] + grad_gain), merged)
    start = (jnp.zeros((D, 3 * inner_width), jnp.float32), jnp.zeros((inner_width, D), jnp.float32), jnp.zeros((D,), jnp.float32))
    totals, merged = lax.scan(step, start, (block_rows, window_index, window_live, cot_blocks))
    return (merged.reshape(device_count * W_DEV * (WIN // 4), 4 * D), totals[0], totals[1], totals[2])
```

```python
import jax
import jax.numpy as jnp
from jax import lax
from jax.experimental import pallas as pl
from jax.experimental.pallas import tpu as pltpu
from jax.sharding import PartitionSpec as P

D = 1280
HEADS = 12
HD = 80
INNER = HEADS * HD
WIN = 64
SLOTS = 8
ROWS = SLOTS * WIN
PAIRS = SLOTS // 2
EPSILON = 1e-06
NEGATIVE = -1e30
SCALE = HD ** (-0.5)
SHARD = 10
HALF = D // 2
BLOCK = HALF // 4
OUT_AT = 2944
GAIN_AT = OUT_AT + INNER
COLS = 3968
MESH = pl.DeviceIdType.MESH
BF = jnp.bfloat16
F32 = jnp.float32


def mm(a, b):
    return lax.dot_general(a, b, (((1,), (0,)), ((), ())), preferred_element_type=F32)


def mm_nt(a, b):
    return lax.dot_general(a, b, (((1,), (1,)), ((), ())), preferred_element_type=F32)


def mm_tn(a, b):
    return lax.dot_general(a, b, (((0,), (0,)), ((), ())), preferred_element_type=F32)


def stack_pair(compact, left):
    zero = jnp.zeros_like(compact)
    return jnp.concatenate(
        [jnp.where(left, compact, zero), jnp.where(left, zero, compact)], axis=0
    ).astype(BF)


def order_rows(lt_ref, slot, tall):
    for core in range(2):
        for a in range(4):
            for b in range(0, 4, 2):
                pieces = []
                for c in (b, b + 1):
                    y, x = (a, c) if slot == 0 else (c, a)
                    at = ((y * 4 + x) * 2 + core) * 40
                    pieces.append(tall[at:at + 40, :])
                to = a * BLOCK + b * 40
                lt_ref[slot, core, to:to + 80, :] = jnp.concatenate(pieces, axis=0).astype(BF)


def local_kernel(
    live_ref, index_ref, patches_ref, cot_ref, gain_ref, wqkv_hbm, wout_hbm,
    merged_ref, lt_ref, rt_ref, gcol_ref,
    wqkv, wout, tall, tall_z, windows, normed, packed, packed_t, probs, att, d_att, merged_rows, d_ctx_t,
    sems,
):
    cp_qkv = pltpu.make_async_copy(wqkv_hbm, wqkv, sems.at[0])
    cp_out = pltpu.make_async_copy(wout_hbm, wout, sems.at[1])
    cp_qkv.start()
    cp_out.start()
    pick_t = (lax.broadcasted_iota(jnp.int32, (ROWS, ROWS), 0) == index_ref[...]).astype(BF)
    picked = mm_tn(pick_t, patches_ref[...])
    windows[...] = picked.astype(BF)
    inverse = lax.rsqrt(jnp.mean(picked * picked, -1, keepdims=True) + EPSILON)
    normed_rows = (picked * inverse).astype(BF)
    normed[...] = normed_rows
    tall[...] = (picked * inverse).T
    order_rows(lt_ref, 0, tall)
    for core in range(2):
        for z in range(4):
            for x in range(4):
                for y in range(4):
                    to = core * HALF + z * BLOCK + x * 40 + y * SHARD
                    at = ((y * 4 + x) * 2 + core) * 40 + z * SHARD
                    tall_z[to:to + SHARD, :] = tall[at:at + SHARD, :]
    for core in range(2):
        lt_ref[1, core] = tall_z[core * HALF:(core + 1) * HALF, :].astype(BF)
    row_i = lax.broadcasted_iota(jnp.int32, (ROWS, ROWS), 0)
    col_i = lax.broadcasted_iota(jnp.int32, (ROWS, ROWS), 1)
    spread = (row_i == (col_i % 128) * 4 + col_i // 128).astype(BF)
    gather = (col_i == (row_i % 128) * 4 + row_i // 128).astype(BF)
    cp_qkv.wait()
    for start, size in ((0, 640), (640, 640), (1280, 640), (1920, 640), (2560, 320)):
        tile = mm(normed_rows, wqkv[:, start:start + size]).astype(BF)
        packed[:, start:start + size] = tile
        packed_t[start:start + size, :] = tile.T

    lane = lax.broadcasted_iota(jnp.int32, (WIN, 128), 1)
    left = lane < WIN
    key_row = lax.broadcasted_iota(jnp.int32, (WIN, 128), 0)

    def forward(pair, carry):
        cols = pl.ds(pl.multiple_of(pair * 128, 128), 128)
        mask = key_row < jnp.where(left, live_ref[0, 2 * pair], live_ref[0, 2 * pair + 1])
        for h in range(HEADS):
            q_t = packed_t[HD * h:HD * (h + 1), cols]
            v_t = packed_t[2 * INNER + HD * h:2 * INNER + HD * (h + 1), cols]
            k_n = packed[cols, INNER + HD * h:INNER + HD * (h + 1)]
            full = mm(k_n, q_t)
            scores = jnp.where(left, full[:WIN], full[WIN:]) * SCALE
            scores = jnp.where(mask, scores, NEGATIVE)
            top = jnp.max(scores, axis=0, keepdims=True)
            weight = jnp.exp(scores - top)
            prob = weight * (1.0 / jnp.sum(weight, axis=0, keepdims=True))
            probs[pair, h] = prob
            rt_ref[OUT_AT + HD * h:OUT_AT + HD * (h + 1), cols] = mm(
                v_t, stack_pair(prob, left)
            ).astype(BF)
        return carry

    lax.fori_loop(0, PAIRS, forward, 0)
    cp_out.wait()
    ctx = rt_ref[OUT_AT:OUT_AT + INNER, :].T
    cot_rows = jnp.concatenate([cot_ref[:, j * D:(j + 1) * D] for j in range(4)], axis=0)
    for n in range(5):
        cols = slice(256 * n, 256 * (n + 1))
        att[:, cols] = mm(ctx, wout[:, cols]) + windows[:, cols].astype(F32)
        d_att[:, cols] = mm(spread, cot_rows[:, cols]).astype(BF)

    gain = gain_ref[...]

    def norm_block(block, total):
        rows = pl.ds(pl.multiple_of(block * WIN, WIN), WIN)
        alive = (
            lax.broadcasted_iota(jnp.int32, (WIN, 1), 0) < live_ref[0, block]
        ).astype(F32)
        attended = att[rows, :]
        inv = lax.rsqrt(jnp.mean(attended * attended, -1, keepdims=True) + EPSILON)
        normalized = attended * inv
        merged_rows[rows, :] = (normalized * gain * alive).astype(BF)
        grad_rows = d_att[rows, :].astype(F32) * alive
        prod = grad_rows * normalized
        scaled = grad_rows * gain
        mean = jnp.mean(scaled * normalized, -1, keepdims=True)
        d_att[rows, :] = (inv * (scaled - normalized * mean)).astype(BF)
        return total + jnp.sum(prod, axis=0, keepdims=True)

    total = lax.fori_loop(0, SLOTS, norm_block, jnp.zeros((1, D), F32))
    d_rows = d_att[...]
    tall[...] = d_rows.astype(F32).T
    order_rows(lt_ref, 2, tall)
    tall[:, :128] = jnp.broadcast_to(total, (128, D)).T
    for core in range(2):
        for x in range(4):
            for y in range(4):
                at = ((y * 4 + x) * 2 + core) * 40
                to = x * BLOCK + y * 40
                gcol_ref[core, to:to + 40, :] = tall[at:at + 40, :128]
    rt_ref[3 * INNER:OUT_AT, :] = jnp.zeros((OUT_AT - 3 * INNER, ROWS), BF)
    rt_ref[OUT_AT + INNER:, :] = jnp.zeros((COLS - OUT_AT - INNER, ROWS), BF)
    for n in range(5):
        cols = slice(256 * n, 256 * (n + 1))
        back = mm(gather, merged_rows[:, cols]).astype(BF)
        for j in range(4):
            merged_ref[:, j * D + 256 * n:j * D + 256 * (n + 1)] = back[128 * j:128 * (j + 1)]
    for n in range(3):
        d_ctx_t[320 * n:320 * (n + 1), :] = mm_nt(wout[320 * n:320 * (n + 1), :], d_rows).astype(BF)

    def backward(pair, carry):
        cols = pl.ds(pl.multiple_of(pair * 128, 128), 128)
        for h in range(HEADS):
            q_t = packed_t[HD * h:HD * (h + 1), cols]
            k_t = packed_t[INNER + HD * h:INNER + HD * (h + 1), cols]
            v_n = packed[cols, 2 * INNER + HD * h:2 * INNER + HD * (h + 1)]
            dc_t = d_ctx_t[HD * h:HD * (h + 1), cols]
            prob = probs[pair, h]
            full = mm(v_n, dc_t)
            d_prob = jnp.where(left, full[:WIN], full[WIN:])
            total = jnp.sum(d_prob * prob, axis=0, keepdims=True)
            d_score = stack_pair(prob * (d_prob - total) * SCALE, left)
            rt_ref[HD * h:HD * (h + 1), cols] = mm(k_t, d_score).astype(BF)
            rt_ref[INNER + HD * h:INNER + HD * (h + 1), cols] = mm_nt(q_t, d_score).astype(BF)
            rt_ref[2 * INNER + HD * h:2 * INNER + HD * (h + 1), cols] = mm_nt(
                dc_t, stack_pair(prob, left)
            ).astype(BF)
        return carry

    lax.fori_loop(0, PAIRS, backward, 0)


def local_call(patches, window_index, window_live, d_merged, w_qkv, w_out, merge_gain):
    vmem = pl.BlockSpec(memory_space=pltpu.VMEM)
    smem = pl.BlockSpec(memory_space=pltpu.SMEM)
    hbm = pl.BlockSpec(memory_space=pl.ANY)
    return pl.pallas_call(
        local_kernel,
        out_shape=(
            jax.ShapeDtypeStruct((ROWS // 4, 4 * D), BF),
            jax.ShapeDtypeStruct((3, 2, HALF, ROWS), BF),
            jax.ShapeDtypeStruct((COLS, ROWS), BF),
            jax.ShapeDtypeStruct((2, HALF, 128), F32),
        ),
        in_specs=[smem, vmem, vmem, vmem, vmem, hbm, hbm],
        out_specs=(vmem, vmem, vmem, vmem),
        scratch_shapes=[
            pltpu.VMEM((D, 3 * INNER), BF),
            pltpu.VMEM((INNER, D), BF),
            pltpu.VMEM((D, ROWS), F32),
            pltpu.VMEM((D, ROWS), F32),
            pltpu.VMEM((ROWS, D), BF),
            pltpu.VMEM((ROWS, D), BF),
            pltpu.VMEM((ROWS, 3 * INNER), BF),
            pltpu.VMEM((3 * INNER, ROWS), BF),
            pltpu.VMEM((PAIRS, HEADS, WIN, 128), F32),
            pltpu.VMEM((ROWS, D), F32),
            pltpu.VMEM((ROWS, D), BF),
            pltpu.VMEM((ROWS, D), BF),
            pltpu.VMEM((INNER, ROWS), BF),
            pltpu.SemaphoreType.DMA((2,)),
        ],
        compiler_params=pltpu.CompilerParams(vmem_limit_bytes=60 * 2**20),
        cost_estimate=pl.CostEstimate(flops=9_000_000_000, bytes_accessed=20_000_000, transcendentals=400_000),
    )(window_live, window_index, patches, d_merged, merge_gain.reshape(1, D), w_qkv, w_out)


PARTS = (
    (2944, 512, 2, "xyz"),
    (0, 768, 0, "yxz"),
    (1408, 768, 1, "zxy"),
    (3456, 512, 2, "xyz"),
    (768, 640, 0, "yxz"),
    (2176, 768, 1, "zxy"),
)
PER_PART = 13


def sum_kernel(lt_ref, rt_ref, gcol_ref, fq_ref, fo_ref, *scratch):
    sends, recvs = scratch[-2:]
    buffers = [scratch[10 * i:10 * (i + 1)] for i in range(len(PARTS))]
    dp = lax.axis_index("dp")
    core = dp % 2
    place = {"x": (dp // 2) % 4, "y": dp // 8, "z": lax.axis_index("vis")}

    def device(axis=None, step=0):
        at = dict(place)
        if axis is not None:
            at[axis] = (at[axis] + step) % 4
        side = 1 - core if axis is None else core
        return {"dp": (at["y"] * 4 + at["x"]) * 2 + side, "vis": at["z"]}

    partners = [device()] + [device(axis, step) for axis in "xyz" for step in (1, 2, 3)]
    barrier = pltpu.get_barrier_semaphore()
    for partner in partners:
        pl.semaphore_signal(barrier, inc=1, device_id=partner, device_id_type=MESH)

    started = {}

    def send(part, number, src, dst, target):
        copy = pltpu.make_async_remote_copy(
            src_ref=src, dst_ref=dst,
            send_sem=sends.at[PER_PART * part + number],
            recv_sem=recvs.at[PER_PART * part + number],
            device_id=target, device_id_type=MESH,
        )
        copy.start()
        started[part, number] = copy

    def arrived(part, number):
        started[part, number].wait_recv()

    def tiles(part):
        width = PARTS[part][1]
        return [(at, min(256, width - at)) for at in range(0, width, 256)]

    def product(part, side, at, size):
        first, width, slot, route = PARTS[part]
        out = mm_nt(lt_ref[slot, side], rt_ref[first + at:first + at + size, :])
        if first + at + size == COLS:
            gain = gcol_ref[side]
            lane = lax.broadcasted_iota(jnp.int32, gain.shape, 1)
            gain = jnp.where(lane >= GAIN_AT % 128, gain, 0.0)
            out = out + jnp.concatenate([jnp.zeros((HALF, size - 128), F32), gain], axis=1)
        return out

    def make_other(part):
        to_pair = buffers[part][0]
        for at, size in tiles(part):
            to_pair[:, at:at + size] = product(part, 1 - core, at, size).astype(BF)

    def send_other(part):
        send(part, 0, buffers[part][0], buffers[part][1], device())

    def make_own(part):
        route = PARTS[part][3]
        from_pair, own, mid, wide = buffers[part][1:5]
        mine = [product(part, core, at, size) for at, size in tiles(part)]
        arrived(part, 0)
        for (at, size), value in zip(tiles(part), mine):
            value = (value + from_pair[:, at:at + size].astype(F32)).astype(BF)
            for b in range(4):
                own[b, :, at:at + size] = value[BLOCK * b:BLOCK * (b + 1)]
        me = place[route[0]]
        up, down, far = (me + 1) % 4, (me + 3) % 4, (me + 2) % 4
        low, high = pl.ds(0, 80), pl.ds(80, 80)
        send(part, 1, own.at[far, low], mid.at[0], device(route[0], 1))
        send(part, 2, own.at[far, high], mid.at[1], device(route[0], 3))
        send(part, 3, own.at[up, high], wide.at[0, high], device(route[0], 1))
        send(part, 4, own.at[down, low], wide.at[1, low], device(route[0], 3))

    def pass_on(part):
        route = PARTS[part][3]
        own, mid, wide, on = buffers[part][2:6]
        me = place[route[0]]
        up, down = (me + 1) % 4, (me + 3) % 4
        arrived(part, 1)
        on[0] = (own[up, :80, :].astype(F32) + mid[0].astype(F32)).astype(BF)
        send(part, 5, on.at[0], wide.at[0, pl.ds(0, 80)], device(route[0], 1))
        arrived(part, 2)
        on[1] = (own[down, 80:, :].astype(F32) + mid[1].astype(F32)).astype(BF)
        send(part, 6, on.at[1], wide.at[1, pl.ds(80, 80)], device(route[0], 3))

    def second(part):
        route = PARTS[part][3]
        own, mid, wide, on, two, two_in = buffers[part][2:8]
        for number in (3, 4, 5, 6):
            arrived(part, number)
        me = place[route[0]]
        value = own[me].astype(F32) + wide[0].astype(F32) + wide[1].astype(F32)
        value = jnp.concatenate([value, jnp.zeros((8, value.shape[1]), F32)], axis=0)
        for b in range(4):
            two[b] = value[40 * b:40 * b + 48].astype(BF)
        for step in (1, 2, 3):
            to = (place[route[1]] + step) % 4
            send(part, 6 + step, two.at[to], two_in.at[step - 1], device(route[1], step))

    def third(part):
        route = PARTS[part][3]
        two, two_in, three, three_in = buffers[part][6:10]
        value = two[place[route[1]]].astype(F32)
        for step in (1, 2, 3):
            arrived(part, 6 + step)
            value = value + two_in[step - 1].astype(F32)
        for b in range(4):
            three[b] = value[SHARD * b:SHARD * b + 16].astype(BF)
        for step in (1, 2, 3):
            to = (place[route[2]] + step) % 4
            send(part, 9 + step, three.at[to], three_in.at[step - 1], device(route[2], step))

    def finish(part):
        first, width, slot, route = PARTS[part]
        three, three_in = buffers[part][8:10]
        value = three[place[route[2]]].astype(F32)
        for step in (1, 2, 3):
            arrived(part, 9 + step)
            value = value + three_in[step - 1].astype(F32)
        if slot == 2:
            fo_ref[first - OUT_AT:first - OUT_AT + width, :] = value.T
        else:
            fq_ref[:, first:first + width] = value

    make_other(0)
    pl.semaphore_wait(barrier, len(partners))
    send_other(0)
    for part in (1, 2):
        make_other(part)
        send_other(part)
    for part in range(6):
        make_own(part)
        if part < 3:
            make_other(part + 3)
            send_other(part + 3)
    for part in range(6):
        pass_on(part)
    for part in range(6):
        second(part)
    for part in range(6):
        third(part)
    for part in range(6):
        finish(part)
    for copy in started.values():
        copy.wait_send()


def sum_call(lt, rt, gcol):
    vmem = pl.BlockSpec(memory_space=pltpu.VMEM)
    scratch = []
    for first, width, slot, route in PARTS:
        scratch += [
            pltpu.VMEM((HALF, width), BF),
            pltpu.VMEM((HALF, width), BF),
            pltpu.VMEM((4, BLOCK, width), BF),
            pltpu.VMEM((2, 80, width), BF),
            pltpu.VMEM((2, BLOCK, width), BF),
            pltpu.VMEM((2, 80, width), BF),
            pltpu.VMEM((4, 48, width), BF),
            pltpu.VMEM((3, 48, width), BF),
            pltpu.VMEM((4, 16, width), BF),
            pltpu.VMEM((3, 16, width), BF),
        ]
    count = PER_PART * len(PARTS)
    return pl.pallas_call(
        sum_kernel,
        out_shape=(
            jax.ShapeDtypeStruct((16, OUT_AT), F32),
            jax.ShapeDtypeStruct((COLS - OUT_AT, 16), F32),
        ),
        in_specs=[vmem] * 3,
        out_specs=(vmem, vmem),
        scratch_shapes=scratch + [pltpu.SemaphoreType.DMA((count,)), pltpu.SemaphoreType.DMA((count,))],
        compiler_params=pltpu.CompilerParams(
            collective_id=0, has_side_effects=True, vmem_limit_bytes=60 * 2**20
        ),
        cost_estimate=pl.CostEstimate(flops=5_000_000_000, bytes_accessed=10_000_000, transcendentals=0),
    )(lt, rt, gcol)


def on_device(patches, window_index, window_live, d_merged, w_qkv, w_out, merge_gain):
    merged, lt, rt, gcol = local_call(
        patches, window_index, window_live, d_merged, w_qkv, w_out, merge_gain
    )
    fq, fo = sum_call(lt, rt, gcol)
    return merged, fq[:SHARD, :3 * INNER], fo[:INNER, :SHARD], fo[INNER, :SHARD]


def solution(mesh):
    both = ("dp", "vis")
    rows = P(both, None)
    return jax.shard_map(
        on_device,
        mesh=mesh,
        in_specs=(rows, rows, rows, rows, P(), P(), P()),
        out_specs=(rows, rows, P(None, both), P(both)),
        check_vma=False,
    )
```

```python
import jax
import jax.numpy as jnp
from jax import lax
from jax.experimental import pallas as pl
from jax.experimental.pallas import tpu as pltpu
from jax.sharding import PartitionSpec as P

D = 1280
HEADS = 12
HD = 80
INNER = HEADS * HD
WIN = 64
SLOTS = 8
ROWS = SLOTS * WIN
PAIRS = SLOTS // 2
EPSILON = 1e-06
NEGATIVE = -1e30
SCALE = HD ** (-0.5)
SHARD = 10
HALF = D // 2
BLOCK = HALF // 4
HEAVY = 8
EARLY_AT = 1024
LATE_AT = EARLY_AT + 3 * HEAVY * HD
LATE_END = LATE_AT + 3 * (HEADS - HEAVY) * HD
COLS = 3968
GAIN_AT = INNER
MESH = pl.DeviceIdType.MESH
BF = jnp.bfloat16
F32 = jnp.float32

ROUTES = ("yxz", "xyz", "zxy")
PARTS = (
    (0, 256, 0),
    (256, 256, 1),
    (512, 512, 2),
    (1024, 768, 0),
    (1792, 512, 1),
    (2304, 640, 2),
    (2944, 256, 0),
    (3200, 256, 1),
    (3456, 512, 2),
)
PER_PART = 13
BUFFERS = 8


def mm(a, b):
    return lax.dot_general(a, b, (((1,), (0,)), ((), ())), preferred_element_type=F32)


def mm_nt(a, b):
    return lax.dot_general(a, b, (((1,), (1,)), ((), ())), preferred_element_type=F32)


def mm_tn(a, b):
    return lax.dot_general(a, b, (((0,), (0,)), ((), ())), preferred_element_type=F32)


def stack_pair(compact, left):
    zero = jnp.zeros_like(compact)
    return jnp.concatenate(
        [jnp.where(left, compact, zero), jnp.where(left, zero, compact)], axis=0
    ).astype(BF)


def folded(width):
    return width % 256 == 0


def second_shape(width):
    return (80, width // 2) if folded(width) else (48, width)


def joined_row(kind, head):
    if head < HEAVY:
        return EARLY_AT + (kind * HEAVY + head) * HD
    return LATE_AT + (kind * (HEADS - HEAVY) + head - HEAVY) * HD


def order_rows(left_ops, operand, tall, tall_z):
    for core in range(2):
        for first in range(4):
            for b in range(0, 4, 2):
                to = first * BLOCK + b * 40
                for route in range(2):
                    pieces = []
                    for c in (b, b + 1):
                        y, x = (first, c) if route == 0 else (c, first)
                        at = ((y * 4 + x) * 2 + core) * 40
                        pieces.append(tall[at:at + 40, :])
                    left_ops[operand, route, core, to:to + 80, :] = jnp.concatenate(
                        pieces, axis=0
                    ).astype(BF)
        for z in range(4):
            for x in range(4):
                for y in range(4):
                    to = core * HALF + z * BLOCK + x * 40 + y * SHARD
                    at = ((y * 4 + x) * 2 + core) * 40 + z * SHARD
                    tall_z[to:to + SHARD, :] = tall[at:at + SHARD, :]
        left_ops[operand, 2, core] = tall_z[core * HALF:(core + 1) * HALF, :].astype(BF)


def main_kernel(
    live_ref, index_ref, gain_ref, patches_hbm, cot_hbm, wqkv_hbm, wout_hbm,
    merged_hbm, final_ref,
    patches, wide_rows, wqkv, wout, tall, tall_z, att, rows_low, packed_t, probs, d_att, d_ctx_t,
    left_ops, right_op, gain_cols, local_sems, *scratch,
):
    sends, recvs = scratch[-2:]
    buffers = [scratch[BUFFERS * i:BUFFERS * (i + 1)] for i in range(len(PARTS))]
    loads = [
        pltpu.make_async_copy(src, dst, local_sems.at[i])
        for i, (src, dst) in enumerate(
            ((patches_hbm, patches), (wqkv_hbm, wqkv), (cot_hbm, wide_rows), (wout_hbm, wout))
        )
    ]
    for load in loads:
        load.start()

    dp = lax.axis_index("dp")
    core = dp % 2
    place = {"x": (dp // 2) % 4, "y": dp // 8, "z": lax.axis_index("vis")}

    def coordinate(at, side):
        return {"dp": (at["y"] * 4 + at["x"]) * 2 + side, "vis": at["z"]}

    pair_device = coordinate(place, 1 - core)
    near = {(axis, step): (place[axis] + step) % 4 for axis in "xyz" for step in (1, 2, 3)}
    devices = {key: coordinate({**place, key[0]: value}, core) for key, value in near.items()}
    barrier = pltpu.get_barrier_semaphore()
    for partner in [pair_device] + list(devices.values()):
        pl.semaphore_signal(barrier, inc=1, device_id=partner, device_id_type=MESH)

    started = {}

    def send(part, number, src, dst, target):
        copy = pltpu.make_async_remote_copy(
            src_ref=src, dst_ref=dst,
            send_sem=sends.at[PER_PART * part + number],
            recv_sem=recvs.at[PER_PART * part + number],
            device_id=target, device_id_type=MESH,
        )
        copy.start()
        started[part, number] = copy

    def arrived(part, number):
        started[part, number].wait_recv()

    def tiles(part):
        width = PARTS[part][1]
        return [(at, min(256, width - at)) for at in range(0, width, 256)]

    def product(part, side, at, size):
        first, width, route = PARTS[part]
        operand = 1 if first < EARLY_AT else 0
        out = mm_nt(left_ops[operand, route, side], right_op[first + at:first + at + size, :])
        if first + at + size == EARLY_AT:
            out = out + jnp.concatenate([jnp.zeros((HALF, size - 128), F32), gain_cols[side]], axis=1)
        return out

    def make_other(part):
        own, from_pair = buffers[part][:2]
        for at, size in tiles(part):
            value = product(part, 1 - core, at, size).astype(BF)
            for b in range(4):
                own[b, :, at:at + size] = value[BLOCK * b:BLOCK * (b + 1)]
        send(part, 0, own, from_pair, pair_device)

    def make_own(part):
        axis = ROUTES[PARTS[part][2]][0]
        own, from_pair, mid, wide = buffers[part][:4]
        started.pop((part, 0)).wait()
        for at, size in tiles(part):
            value = product(part, core, at, size)
            for b in range(4):
                own[b, :, at:at + size] = (
                    value[BLOCK * b:BLOCK * (b + 1)] + from_pair[b, :, at:at + size].astype(F32)
                ).astype(BF)
        up, far, down = (near[axis, step] for step in (1, 2, 3))
        low, high = pl.ds(0, 80), pl.ds(80, 80)
        send(part, 1, own.at[far, low], mid.at[0], devices[axis, 1])
        send(part, 2, own.at[far, high], mid.at[1], devices[axis, 3])
        send(part, 3, own.at[up, high], wide.at[0, high], devices[axis, 1])
        send(part, 4, own.at[down, low], wide.at[1, low], devices[axis, 3])

    def pass_on(part):
        axis = ROUTES[PARTS[part][2]][0]
        own, from_pair, mid, wide = buffers[part][:4]
        up, down = near[axis, 1], near[axis, 3]
        low, high = pl.ds(0, 80), pl.ds(80, 80)
        arrived(part, 1)
        own[up, low, :] = (own[up, low, :].astype(F32) + mid[0].astype(F32)).astype(BF)
        send(part, 5, own.at[up, low], wide.at[0, low], devices[axis, 1])
        arrived(part, 2)
        own[down, high, :] = (own[down, high, :].astype(F32) + mid[1].astype(F32)).astype(BF)
        send(part, 6, own.at[down, high], wide.at[1, high], devices[axis, 3])

    def second(part):
        first, width, route = PARTS[part]
        axis = ROUTES[route][1]
        own, from_pair, mid, wide, two, two_in = buffers[part][:6]
        for number in (3, 4, 5, 6):
            arrived(part, number)
        value = own[place[ROUTES[route][0]]].astype(F32) + wide[0].astype(F32) + wide[1].astype(F32)
        if folded(width):
            for b in range(4):
                rows = value[40 * b:40 * (b + 1)]
                two[b] = jnp.concatenate(
                    [rows[:, :width // 2], rows[:, width // 2:]], axis=0
                ).astype(BF)
        else:
            value = jnp.concatenate([value, jnp.zeros((8, width), F32)], axis=0)
            for b in range(4):
                two[b] = value[40 * b:40 * b + 48].astype(BF)
        for step in (1, 2, 3):
            send(part, 6 + step, two.at[near[axis, step]], two_in.at[step - 1], devices[axis, step])

    def third(part):
        first, width, route = PARTS[part]
        axis = ROUTES[route][2]
        two, two_in, three, three_in = buffers[part][4:8]
        value = two[place[ROUTES[route][1]]].astype(F32)
        for step in (1, 2, 3):
            arrived(part, 6 + step)
            value = value + two_in[step - 1].astype(F32)
        if folded(width):
            value = jnp.concatenate([value[:40], value[40:]], axis=1)
            value = jnp.concatenate([value, jnp.zeros((8, width), F32)], axis=0)
        for b in range(4):
            three[b] = value[SHARD * b:SHARD * b + 16].astype(BF)
        for step in (1, 2, 3):
            send(part, 9 + step, three.at[near[axis, step]], three_in.at[step - 1], devices[axis, step])

    def finish(part):
        first, width, route = PARTS[part]
        three, three_in = buffers[part][6:8]
        value = three[place[ROUTES[route][2]]].astype(F32)
        for step in (1, 2, 3):
            arrived(part, 9 + step)
            value = value + three_in[step - 1].astype(F32)
        final_ref[:, first:first + width] = value

    pick_t = (lax.broadcasted_iota(jnp.int32, (ROWS, ROWS), 0) == index_ref[...]).astype(BF)
    pick = pick_t.T
    loads[0].wait()
    for n in range(5):
        cols = slice(256 * n, 256 * (n + 1))
        att[:, cols] = mm(pick, patches[:, cols])
    for n in range(SLOTS):
        rows = slice(WIN * n, WIN * (n + 1))
        picked = att[rows, :]
        normed = picked * lax.rsqrt(jnp.mean(picked * picked, -1, keepdims=True) + EPSILON)
        rows_low[rows, :] = normed.astype(BF)
    for n in range(5):
        cols = slice(256 * n, 256 * (n + 1))
        tall[cols, :] = rows_low[:, cols].astype(F32).T
    order_rows(left_ops, 0, tall, tall_z)
    right_op[INNER:EARLY_AT, :] = jnp.zeros((EARLY_AT - INNER, ROWS), BF)
    right_op[LATE_END:, :] = jnp.zeros((COLS - LATE_END, ROWS), BF)

    loads[1].wait()
    for n in range(6):
        rows = slice(480 * n, 480 * (n + 1))
        packed_t[rows, :] = mm_nt(wqkv[rows, :], rows_low[...]).astype(BF)

    left = lax.broadcasted_iota(jnp.int32, (WIN, 128), 1) < WIN
    key_row = lax.broadcasted_iota(jnp.int32, (WIN, 128), 0)
    masks = [
        key_row < jnp.where(left, live_ref[0, 2 * pair], live_ref[0, 2 * pair + 1])
        for pair in range(PAIRS)
    ]

    def head_rows(kind, h):
        start = kind * INNER + HD * h
        return slice(start, start + HD) if isinstance(h, int) else pl.ds(pl.multiple_of(start, 16), HD)

    def forward(step, carry):
        todo = [
            (step * 3 + i, pair, slice(128 * pair, 128 * (pair + 1)))
            for i in range(3) for pair in range(PAIRS)
        ]
        fulls = [mm_tn(packed_t[head_rows(1, h), c], packed_t[head_rows(0, h), c]) for h, pair, c in todo]
        stacks = []
        for (h, pair, c), full in zip(todo, fulls):
            scores = jnp.where(left, full[:WIN], full[WIN:]) * SCALE
            scores = jnp.where(masks[pair], scores, NEGATIVE)
            top = jnp.max(scores, axis=0, keepdims=True)
            weight = jnp.exp(scores - top)
            prob = weight * (1.0 / jnp.sum(weight, axis=0, keepdims=True))
            probs[pair, h] = prob
            stacks.append(stack_pair(prob, left))
        for (h, pair, c), stack in zip(todo, stacks):
            right_op[head_rows(0, h), c] = mm(packed_t[head_rows(2, h), c], stack).astype(BF)
        return carry

    lax.fori_loop(0, HEADS // 3, forward, 0)

    row_i = lax.broadcasted_iota(jnp.int32, (ROWS, ROWS), 0)
    col_i = lax.broadcasted_iota(jnp.int32, (ROWS, ROWS), 1)
    spread = (row_i == (col_i % 128) * 4 + col_i // 128).astype(BF)
    gather = (col_i == (row_i % 128) * 4 + row_i // 128).astype(BF)
    loads[2].wait()
    loads[3].wait()
    ctx = right_op[:INNER, :].T
    for n in range(5):
        cols = slice(256 * n, 256 * (n + 1))
        att[:, cols] += mm(ctx, wout[:, cols])
        cot = jnp.concatenate(
            [wide_rows[:, j * D + 256 * n:j * D + 256 * (n + 1)] for j in range(4)], axis=0
        )
        d_att[:, cols] = mm(spread, cot).astype(BF)
    gain = gain_ref[...].reshape(1, D)

    def norm_block(block, total):
        rows = pl.ds(pl.multiple_of(block * WIN, WIN), WIN)
        alive = (
            lax.broadcasted_iota(jnp.int32, (WIN, 1), 0) < live_ref[0, block]
        ).astype(F32)
        attended = att[rows, :]
        inv = lax.rsqrt(jnp.mean(attended * attended, -1, keepdims=True) + EPSILON)
        normalized = attended * inv
        rows_low[rows, :] = (normalized * gain * alive).astype(BF)
        grad_rows = d_att[rows, :].astype(F32) * alive
        prod = grad_rows * normalized
        scaled = grad_rows * gain
        mean = jnp.mean(scaled * normalized, -1, keepdims=True)
        d_att[rows, :] = (inv * (scaled - normalized * mean)).astype(BF)
        return total + jnp.sum(prod, axis=0, keepdims=True)

    total = lax.fori_loop(0, SLOTS, norm_block, jnp.zeros((1, D), F32))
    tall[:, :128] = jnp.broadcast_to(total, (128, D)).T
    lane = lax.broadcasted_iota(jnp.int32, (SHARD, 128), 1)
    for side in range(2):
        for z in range(4):
            for x in range(4):
                for y in range(4):
                    to = z * BLOCK + x * 40 + y * SHARD
                    at = ((y * 4 + x) * 2 + side) * 40 + z * SHARD
                    gain_cols[side, to:to + SHARD, :] = jnp.where(
                        lane >= GAIN_AT % 128, tall[at:at + SHARD, :128], 0.0
                    )
    for n in range(5):
        cols = slice(256 * n, 256 * (n + 1))
        tall[cols, :] = d_att[:, cols].astype(F32).T
    order_rows(left_ops, 1, tall, tall_z)

    pl.semaphore_wait(barrier, 1 + len(devices))
    for part in (0, 1, 2):
        make_other(part)
    for n in range(3):
        rows = slice(320 * n, 320 * (n + 1))
        d_ctx_t[rows, :] = mm_nt(wout[rows, :], d_att[...]).astype(BF)
    for part in (0, 1, 2):
        make_own(part)
    for n in range(5):
        back = mm(gather, rows_low[:, 256 * n:256 * (n + 1)]).astype(BF)
        for j in range(4):
            wide_rows[:, j * D + 256 * n:j * D + 256 * (n + 1)] = back[128 * j:128 * (j + 1)]
    store = pltpu.make_async_copy(wide_rows, merged_hbm, local_sems.at[4])
    store.start()

    def backward(heads):
        todo = [
            (h, pair, slice(128 * pair, 128 * (pair + 1))) for h in heads for pair in range(PAIRS)
        ]
        dcs = [d_ctx_t[head_rows(0, h), c] for h, pair, c in todo]
        fulls = [mm_tn(packed_t[head_rows(2, h), c], dc) for (h, pair, c), dc in zip(todo, dcs)]
        stacks = []
        for (h, pair, c), full in zip(todo, fulls):
            prob = probs[pair, h]
            d_prob = jnp.where(left, full[:WIN], full[WIN:])
            dot = jnp.sum(d_prob * prob, axis=0, keepdims=True)
            stacks.append(stack_pair(prob * (d_prob - dot) * SCALE, left))
        for (h, pair, c), dc in zip(todo, dcs):
            to = joined_row(2, h)
            right_op[to:to + HD, c] = mm_nt(dc, stack_pair(probs[pair, h], left)).astype(BF)
        for (h, pair, c), stack in zip(todo, stacks):
            to = joined_row(0, h)
            right_op[to:to + HD, c] = mm(packed_t[head_rows(1, h), c], stack).astype(BF)
            to = joined_row(1, h)
            right_op[to:to + HD, c] = mm_nt(packed_t[head_rows(0, h), c], stack).astype(BF)

    backward(range(0, 4))
    for part in (0, 1, 2):
        pass_on(part)
    backward(range(4, 8))
    for part in (3, 4, 5):
        make_other(part)
    for part in (0, 1, 2):
        second(part)
    backward(range(8, 12))
    for part in (3, 4, 5):
        make_own(part)
    for part in (6, 7, 8):
        make_other(part)
    for part in (0, 1, 2):
        third(part)
    for part in (6, 7, 8):
        make_own(part)
    for part in (3, 4, 5):
        pass_on(part)
    for part in (0, 1, 2):
        finish(part)
    for part in (6, 7, 8):
        pass_on(part)
    for step in (second, third, finish):
        for part in range(3, 9):
            step(part)
    for copy in started.values():
        copy.wait_send()
    store.wait()


def last_kernel(final_ref, merged_in, merged_ref, qkv_ref, out_ref, gain_ref):
    merged_ref[...] = merged_in[...]
    early, late = HEAVY * HD, (HEADS - HEAVY) * HD
    pieces = []
    for kind in range(3):
        at = EARLY_AT + kind * early
        pieces.append(final_ref[:, at:at + early])
        at = LATE_AT + kind * late
        pieces.append(final_ref[:, at:at + late])
    qkv_ref[...] = jnp.concatenate(pieces, axis=1)[:SHARD]
    out_ref[...] = final_ref[:SHARD, :INNER]
    gain_ref[...] = final_ref[:, EARLY_AT - 128:EARLY_AT].T[GAIN_AT % 128:GAIN_AT % 128 + 1, :SHARD]


def on_device(patches, window_index, window_live, d_merged, w_qkv, w_out, merge_gain):
    vmem = pl.BlockSpec(memory_space=pltpu.VMEM)
    smem = pl.BlockSpec(memory_space=pltpu.SMEM)
    hbm = pl.BlockSpec(memory_space=pl.ANY)
    scratch = [
        pltpu.VMEM((ROWS, D), BF),
        pltpu.VMEM((ROWS // 4, 4 * D), BF),
        pltpu.VMEM((3 * INNER, D), BF),
        pltpu.VMEM((INNER, D), BF),
        pltpu.VMEM((D, ROWS), F32),
        pltpu.VMEM((D, ROWS), F32),
        pltpu.VMEM((ROWS, D), F32),
        pltpu.VMEM((ROWS, D), BF),
        pltpu.VMEM((3 * INNER, ROWS), BF),
        pltpu.VMEM((PAIRS, HEADS, WIN, 128), F32),
        pltpu.VMEM((ROWS, D), BF),
        pltpu.VMEM((INNER, ROWS), BF),
        pltpu.VMEM((2, 3, 2, HALF, ROWS), BF),
        pltpu.VMEM((COLS, ROWS), BF),
        pltpu.VMEM((2, HALF, 128), F32),
        pltpu.SemaphoreType.DMA((5,)),
    ]
    for first, width, route in PARTS:
        shape = second_shape(width)
        scratch += [
            pltpu.VMEM((4, BLOCK, width), BF),
            pltpu.VMEM((4, BLOCK, width), BF),
            pltpu.VMEM((2, 80, width), BF),
            pltpu.VMEM((2, BLOCK, width), BF),
            pltpu.VMEM((4,) + shape, BF),
            pltpu.VMEM((3,) + shape, BF),
            pltpu.VMEM((4, 16, width), BF),
            pltpu.VMEM((3, 16, width), BF),
        ]
    count = PER_PART * len(PARTS)
    scratch += [pltpu.SemaphoreType.DMA((count,)), pltpu.SemaphoreType.DMA((count,))]
    merged, final = pl.pallas_call(
        main_kernel,
        out_shape=(
            jax.ShapeDtypeStruct((ROWS // 4, 4 * D), BF),
            jax.ShapeDtypeStruct((16, COLS), F32),
        ),
        in_specs=[smem, vmem, vmem, hbm, hbm, hbm, hbm],
        out_specs=(hbm, vmem),
        scratch_shapes=scratch,
        compiler_params=pltpu.CompilerParams(
            collective_id=0, has_side_effects=True, vmem_limit_bytes=62 * 2**20
        ),
        cost_estimate=pl.CostEstimate(
            flops=14_000_000_000, bytes_accessed=14_000_000, transcendentals=400_000
        ),
    )(window_live, window_index, merge_gain, patches, d_merged, w_qkv.T, w_out)
    merged, qkv, out, gain = pl.pallas_call(
        last_kernel,
        out_shape=(
            jax.ShapeDtypeStruct((ROWS // 4, 4 * D), BF),
            jax.ShapeDtypeStruct((SHARD, 3 * INNER), F32),
            jax.ShapeDtypeStruct((SHARD, INNER), F32),
            jax.ShapeDtypeStruct((1, SHARD), F32),
        ),
        in_specs=[vmem, vmem],
        out_specs=(vmem, vmem, vmem, vmem),
    )(final, merged)
    return merged, qkv, out.T, gain.reshape(SHARD)


def solution(mesh):
    both = ("dp", "vis")
    rows = P(both, None)
    return jax.shard_map(
        on_device,
        mesh=mesh,
        in_specs=(rows, rows, rows, rows, P(), P(), P()),
        out_specs=(rows, rows, P(None, both), P(both)),
        check_vma=False,
    )
```

```python
import functools

import jax
import jax.numpy as jnp
from jax import lax
from jax.experimental import pallas as pl
from jax.experimental.pallas import tpu as pltpu
from jax.sharding import PartitionSpec as P

D = 1280
HEADS = 12
HD = 80
INNER = HEADS * HD
WIN = 64
SLOTS = 8
ROWS = SLOTS * WIN
PAIRS = SLOTS // 2
EPSILON = 1e-06
NEGATIVE = -1e30
SCALE = HD ** (-0.5)
SHARD = 10
HALF = D // 2
BLOCK = HALF // 4
GROUPS = ((0, 1024), (1024, 2560), (2560, 3584), (3584, 4096))
GROUP_HEADS = ((0, 0), (0, 6), (6, 10), (10, 12))
GROUP_ENDS = tuple(end for _, end in GROUPS)
COLS = 4096
OUT_END = GROUPS[0][1]
GAIN_AT = INNER
MESH = pl.DeviceIdType.MESH
BF = jnp.bfloat16
F32 = jnp.float32

ROUTES = ("yxz", "xyz", "zxy")
PARTS = (
    (0, 256, 0), (256, 256, 1), (512, 512, 2),
    (1024, 512, 0), (1536, 512, 1), (2048, 512, 2),
    (2560, 512, 0), (3072, 256, 1), (3328, 256, 2),
    (3584, 256, 0), (3840, 256, 2),
)
PER_PART = 13
BUFFERS = 8


def mm(a, b):
    return lax.dot_general(a, b, (((1,), (0,)), ((), ())), preferred_element_type=F32)


def mm_nt(a, b):
    return lax.dot_general(a, b, (((1,), (1,)), ((), ())), preferred_element_type=F32)


def mm_tn(a, b):
    return lax.dot_general(a, b, (((0,), (0,)), ((), ())), preferred_element_type=F32)


def stack_pair(compact, left):
    zero = jnp.zeros_like(compact)
    return jnp.concatenate(
        [jnp.where(left, compact, zero), jnp.where(left, zero, compact)], axis=0
    ).astype(BF)


def folded(width):
    return width % 256 == 0


def second_shape(width):
    return (80, width // 2) if folded(width) else (48, width)


def joined_row(kind, head):
    for (start, _), (first, end) in zip(GROUPS, GROUP_HEADS):
        if first <= head < end:
            return start + (kind * (end - first) + head - first) * HD


def order_rows(left_ops, operand, tall, core, first):
    for b in range(0, 4, 2):
        to = first * BLOCK + b * 40
        for route in range(2):
            pieces = []
            for c in (b, b + 1):
                y, x = (first, c) if route == 0 else (c, first)
                at = ((y * 4 + x) * 2 + core) * 40
                pieces.append(tall[at:at + 40, :])
            left_ops[operand, route, core, to:to + 80, :] = jnp.concatenate(
                pieces, axis=0
            ).astype(BF)


def order_rows_z(left_ops, operand, tall, tall_z, core, z):
    for x in range(4):
        for y in range(4):
            to = core * HALF + z * BLOCK + x * 40 + y * SHARD
            at = ((y * 4 + x) * 2 + core) * 40 + z * SHARD
            tall_z[to:to + SHARD, :] = tall[at:at + SHARD, :]
    to = z * BLOCK
    left_ops[operand, 2, core, to:to + BLOCK] = tall_z[
        core * HALF + to:core * HALF + to + BLOCK, :
    ].astype(BF)


def main_kernel(
    live_hbm, index_hbm, gain_hbm, patches_hbm, cot_hbm, wqkv_hbm, wout_hbm,
    merged_hbm, final_hbm,
    live_ref, index_ref, gain_ref, final_ref,
    patches, wide_rows, wqkv, wout, tall, tall_z, att, rows_low, packed_t, probs, d_att, d_ctx_t,
    left_ops, right_op, gain_cols, local_sems, *scratch,
):
    sends, recvs = scratch[-2:]
    buffers = [scratch[BUFFERS * i:BUFFERS * (i + 1)] for i in range(len(PARTS))]
    loads = [
        pltpu.make_async_copy(src, dst, local_sems.at[i])
        for i, (src, dst) in enumerate(
            [(index_hbm, index_ref), (patches_hbm, patches), (live_hbm, live_ref), (gain_hbm, gain_ref)]
            + [(cot_hbm, wide_rows)]
            + [(wqkv_hbm.at[pl.ds(480 * n, 480)], wqkv.at[pl.ds(480 * n, 480)]) for n in range(6)]
            + [(wout_hbm, wout)]
        )
    ]
    for load in loads:
        load.start()

    dp = lax.axis_index("dp")
    core = dp % 2
    place = {"x": (dp // 2) % 4, "y": dp // 8, "z": lax.axis_index("vis")}

    def coordinate(at, side):
        return {"dp": (at["y"] * 4 + at["x"]) * 2 + side, "vis": at["z"]}

    pair_device = coordinate(place, 1 - core)
    near = {(axis, step): (place[axis] + step) % 4 for axis in "xyz" for step in (1, 2, 3)}
    devices = {key: coordinate({**place, key[0]: value}, core) for key, value in near.items()}
    barrier = pltpu.get_barrier_semaphore()
    for partner in [pair_device] + list(devices.values()):
        pl.semaphore_signal(barrier, inc=1, device_id=partner, device_id_type=MESH)

    started = {}
    stored = []

    def send(part, number, src, dst, target):
        copy = pltpu.make_async_remote_copy(
            src_ref=src, dst_ref=dst,
            send_sem=sends.at[PER_PART * part + number],
            recv_sem=recvs.at[PER_PART * part + number],
            device_id=target, device_id_type=MESH,
        )
        copy.start()
        started[part, number] = copy

    def arrived(part, number):
        started[part, number].wait_recv()

    def tiles(part):
        width = PARTS[part][1]
        return [(at, min(256, width - at)) for at in range(0, width, 256)]

    def product(part, side, at, size):
        first, width, route = PARTS[part]
        operand = 1 if first < OUT_END else 0
        out = mm_nt(left_ops[operand, route, side], right_op[first + at:first + at + size, :])
        if first + at + size == OUT_END:
            out = out + jnp.concatenate([jnp.zeros((HALF, size - 128), F32), gain_cols[side]], axis=1)
        return out

    def make_other(part):
        own, from_pair = buffers[part][:2]
        for at, size in tiles(part):
            value = product(part, 1 - core, at, size).astype(BF)
            for b in range(4):
                own[b, :, at:at + size] = value[BLOCK * b:BLOCK * (b + 1)]
        send(part, 0, own, from_pair, pair_device)

    def make_own(part):
        axis = ROUTES[PARTS[part][2]][0]
        own, from_pair, mid, wide = buffers[part][:4]
        started.pop((part, 0)).wait()
        for at, size in tiles(part):
            value = product(part, core, at, size)
            for b in range(4):
                own[b, :, at:at + size] = (
                    value[BLOCK * b:BLOCK * (b + 1)] + from_pair[b, :, at:at + size].astype(F32)
                ).astype(BF)
        up, far, down = (near[axis, step] for step in (1, 2, 3))
        low, high = pl.ds(0, 80), pl.ds(80, 80)
        send(part, 1, own.at[far, low], mid.at[0], devices[axis, 1])
        send(part, 2, own.at[far, high], mid.at[1], devices[axis, 3])
        send(part, 3, own.at[up, high], wide.at[0, high], devices[axis, 1])
        send(part, 4, own.at[down, low], wide.at[1, low], devices[axis, 3])

    def pass_on(part):
        axis = ROUTES[PARTS[part][2]][0]
        own, from_pair, mid, wide = buffers[part][:4]
        up, down = near[axis, 1], near[axis, 3]
        low, high = pl.ds(0, 80), pl.ds(80, 80)
        arrived(part, 1)
        own[up, low, :] = (own[up, low, :].astype(F32) + mid[0].astype(F32)).astype(BF)
        send(part, 5, own.at[up, low], wide.at[0, low], devices[axis, 1])
        arrived(part, 2)
        own[down, high, :] = (own[down, high, :].astype(F32) + mid[1].astype(F32)).astype(BF)
        send(part, 6, own.at[down, high], wide.at[1, high], devices[axis, 3])

    def second(part):
        first, width, route = PARTS[part]
        axis = ROUTES[route][1]
        own, from_pair, mid, wide, two, two_in = buffers[part][:6]
        for number in (3, 4, 5, 6):
            arrived(part, number)
        value = own[place[ROUTES[route][0]]].astype(F32) + wide[0].astype(F32) + wide[1].astype(F32)
        if folded(width):
            for b in range(4):
                rows = value[40 * b:40 * (b + 1)]
                two[b] = jnp.concatenate(
                    [rows[:, :width // 2], rows[:, width // 2:]], axis=0
                ).astype(BF)
        else:
            value = jnp.concatenate([value, jnp.zeros((8, width), F32)], axis=0)
            for b in range(4):
                two[b] = value[40 * b:40 * b + 48].astype(BF)
        for step in (1, 2, 3):
            send(part, 6 + step, two.at[near[axis, step]], two_in.at[step - 1], devices[axis, step])

    def third(part):
        first, width, route = PARTS[part]
        axis = ROUTES[route][2]
        two, two_in, three, three_in = buffers[part][4:8]
        value = two[place[ROUTES[route][1]]].astype(F32)
        for step in (1, 2, 3):
            arrived(part, 6 + step)
            value = value + two_in[step - 1].astype(F32)
        if folded(width):
            value = jnp.concatenate([value[:40], value[40:]], axis=1)
            value = jnp.concatenate([value, jnp.zeros((8, width), F32)], axis=0)
        for b in range(4):
            three[b] = value[SHARD * b:SHARD * b + 16].astype(BF)
        for step in (1, 2, 3):
            send(part, 9 + step, three.at[near[axis, step]], three_in.at[step - 1], devices[axis, step])

    def finish(part):
        first, width, route = PARTS[part]
        three, three_in = buffers[part][6:8]
        value = three[place[ROUTES[route][2]]].astype(F32)
        for step in (1, 2, 3):
            arrived(part, 9 + step)
            value = value + three_in[step - 1].astype(F32)
        final_ref[:, first:first + width] = value
        if first + width in GROUP_ENDS:
            group = GROUP_ENDS.index(first + width)
            cols = pl.ds(GROUPS[group][0], first + width - GROUPS[group][0])
            copy = pltpu.make_async_copy(
                final_ref.at[:, cols], final_hbm.at[:, cols], local_sems.at[13 + group]
            )
            copy.start()
            stored.append(copy)

    loads[0].wait()
    pick_t = (lax.broadcasted_iota(jnp.int32, (ROWS, ROWS), 0) == index_ref[...]).astype(BF)
    pick = pick_t.T
    loads[1].wait()
    for n in range(5):
        cols = slice(256 * n, 256 * (n + 1))
        att[:, cols] = mm(pick, patches[:, cols])
    row_i = lax.broadcasted_iota(jnp.int32, (ROWS, ROWS), 0)
    col_i = lax.broadcasted_iota(jnp.int32, (ROWS, ROWS), 1)
    spread = (row_i == (col_i % 128) * 4 + col_i // 128).astype(BF)
    loads[4].wait()
    for n in range(5):
        cols = slice(256 * n, 256 * (n + 1))
        cot = jnp.concatenate(
            [wide_rows[:, j * D + 256 * n:j * D + 256 * (n + 1)] for j in range(4)], axis=0
        )
        d_att[:, cols] = mm(spread, cot).astype(BF)
    for n in range(SLOTS):
        rows = slice(WIN * n, WIN * (n + 1))
        picked = att[rows, :]
        normed = picked * lax.rsqrt(jnp.mean(picked * picked, -1, keepdims=True) + EPSILON)
        rows_low[rows, :] = normed.astype(BF)
    for (start, end), (first, last) in zip(GROUPS, GROUP_HEADS):
        used = start + (3 * HD * (last - first) or INNER)
        right_op[used:end, :] = jnp.zeros((end - used, ROWS), BF)

    def turn(source, n):
        cols = slice(256 * n, 256 * (n + 1))
        tall[cols, :] = source[:, cols].astype(F32).T

    corners = [(core, first) for core in range(2) for first in range(4)]
    beside = [functools.partial(turn, rows_low, n) for n in range(5)]
    beside += [functools.partial(order_rows, left_ops, 0, tall, *corner) for corner in corners]
    beside += [functools.partial(order_rows_z, left_ops, 0, tall, tall_z, *corner) for corner in corners]
    for n in range(6):
        rows = slice(480 * n, 480 * (n + 1))
        loads[5 + n].wait()
        packed_t[rows, :] = mm_nt(wqkv[rows, :], rows_low[...]).astype(BF)
        for piece in beside[4 * n:4 * n + 4]:
            piece()

    loads[2].wait()
    loads[3].wait()
    left = lax.broadcasted_iota(jnp.int32, (WIN, 128), 1) < WIN
    key_row = lax.broadcasted_iota(jnp.int32, (WIN, 128), 0)
    masks = [
        key_row < jnp.where(left, live_ref[0, 2 * pair], live_ref[0, 2 * pair + 1])
        for pair in range(PAIRS)
    ]

    def head_rows(kind, h):
        start = kind * INNER + HD * h
        return slice(start, start + HD) if isinstance(h, int) else pl.ds(pl.multiple_of(start, 16), HD)

    def forward(step, carry):
        todo = [
            (step * 3 + i, pair, slice(128 * pair, 128 * (pair + 1)))
            for i in range(3) for pair in range(PAIRS)
        ]
        fulls = [mm_tn(packed_t[head_rows(1, h), c], packed_t[head_rows(0, h), c]) for h, pair, c in todo]
        stacks = []
        for (h, pair, c), full in zip(todo, fulls):
            scores = jnp.where(left, full[:WIN], full[WIN:]) * SCALE
            scores = jnp.where(masks[pair], scores, NEGATIVE)
            top = jnp.max(scores, axis=0, keepdims=True)
            weight = jnp.exp(scores - top)
            prob = weight * (1.0 / jnp.sum(weight, axis=0, keepdims=True))
            probs[pair, h] = prob
            stacks.append(stack_pair(prob, left))
        for (h, pair, c), stack in zip(todo, stacks):
            right_op[head_rows(0, h), c] = mm(packed_t[head_rows(2, h), c], stack).astype(BF)
        return carry

    lax.fori_loop(0, HEADS // 3, forward, 0)

    loads[11].wait()
    ctx = right_op[:INNER, :].T
    for n in range(5):
        cols = slice(256 * n, 256 * (n + 1))
        att[:, cols] += mm(ctx, wout[:, cols])
    gain = gain_ref[...].reshape(1, D)

    def norm_block(block, total):
        rows = pl.ds(pl.multiple_of(block * WIN, WIN), WIN)
        alive = (
            lax.broadcasted_iota(jnp.int32, (WIN, 1), 0) < live_ref[0, block]
        ).astype(F32)
        attended = att[rows, :]
        inv = lax.rsqrt(jnp.mean(attended * attended, -1, keepdims=True) + EPSILON)
        normalized = attended * inv
        patches[rows, :] = (normalized * gain * alive).astype(BF)
        grad_rows = d_att[rows, :].astype(F32) * alive
        prod = grad_rows * normalized
        scaled = grad_rows * gain
        mean = jnp.mean(scaled * normalized, -1, keepdims=True)
        d_att[rows, :] = (inv * (scaled - normalized * mean)).astype(BF)
        return total + jnp.sum(prod, axis=0, keepdims=True)

    total = lax.fori_loop(0, SLOTS, norm_block, jnp.zeros((1, D), F32))
    for n in range(5):
        turn(d_att, n)
    for corner in corners:
        order_rows(left_ops, 1, tall, *corner)
    pl.semaphore_wait(barrier, 1 + len(devices))
    make_other(0)
    make_other(1)
    for corner in corners:
        order_rows_z(left_ops, 1, tall, tall_z, *corner)
    tall[:, :128] = jnp.broadcast_to(total, (128, D)).T
    lane = lax.broadcasted_iota(jnp.int32, (SHARD, 128), 1)
    for side in range(2):
        for z in range(4):
            for x in range(4):
                for y in range(4):
                    to = z * BLOCK + x * 40 + y * SHARD
                    at = ((y * 4 + x) * 2 + side) * 40 + z * SHARD
                    gain_cols[side, to:to + SHARD, :] = jnp.where(
                        lane >= GAIN_AT % 128, tall[at:at + SHARD, :128], 0.0
                    )
    make_other(2)
    for n in range(3):
        rows = slice(320 * n, 320 * (n + 1))
        d_ctx_t[rows, :] = mm_nt(wout[rows, :], d_att[...]).astype(BF)
    def backward(heads):
        todo = [
            (h, pair, slice(128 * pair, 128 * (pair + 1))) for h in heads for pair in range(PAIRS)
        ]
        dcs = [d_ctx_t[head_rows(0, h), c] for h, pair, c in todo]
        fulls = [mm_tn(packed_t[head_rows(2, h), c], dc) for (h, pair, c), dc in zip(todo, dcs)]
        stacks = []
        for (h, pair, c), full in zip(todo, fulls):
            prob = probs[pair, h]
            d_prob = jnp.where(left, full[:WIN], full[WIN:])
            dot = jnp.sum(d_prob * prob, axis=0, keepdims=True)
            stacks.append(stack_pair(prob * (d_prob - dot) * SCALE, left))
        for (h, pair, c), dc in zip(todo, dcs):
            to = joined_row(2, h)
            right_op[to:to + HD, c] = mm_nt(dc, stack_pair(probs[pair, h], left)).astype(BF)
        for (h, pair, c), stack in zip(todo, stacks):
            to = joined_row(0, h)
            right_op[to:to + HD, c] = mm(packed_t[head_rows(1, h), c], stack).astype(BF)
            to = joined_row(1, h)
            right_op[to:to + HD, c] = mm_nt(packed_t[head_rows(0, h), c], stack).astype(BF)

    def each(step, group):
        start, end = GROUPS[group]
        for part, (first, width, route) in enumerate(PARTS):
            if start <= first < end:
                step(part)

    each(make_own, 0)
    backward(range(0, 6))
    each(make_other, 1)
    backward(range(6, 10))
    each(make_own, 1)
    each(make_other, 2)
    backward(range(10, 12))
    each(pass_on, 0)
    each(make_own, 2)
    each(make_other, 3)
    gather = (col_i == (row_i % 128) * 4 + row_i // 128).astype(BF)
    for n in range(5):
        back = mm(gather, patches[:, 256 * n:256 * (n + 1)]).astype(BF)
        for j in range(4):
            wide_rows[:, j * D + 256 * n:j * D + 256 * (n + 1)] = back[128 * j:128 * (j + 1)]
    store = pltpu.make_async_copy(wide_rows, merged_hbm, local_sems.at[12])
    store.start()

    each(make_own, 3)
    each(second, 0)
    for group in (1, 2, 3):
        each(pass_on, group)
    each(third, 0)
    for group in (1, 2, 3):
        each(second, group)
    each(finish, 0)
    for step in (third, finish):
        for group in (1, 2, 3):
            each(step, group)
    for copy in started.values():
        copy.wait_send()
    for copy in stored + [store]:
        copy.wait()


def last_kernel(final_ref, merged_in, merged_ref, qkv_ref, out_ref, gain_ref):
    merged_ref[...] = merged_in[...]
    pieces = []
    for kind in range(3):
        for (start, _), (first, end) in zip(GROUPS[1:], GROUP_HEADS[1:]):
            width = HD * (end - first)
            pieces.append(final_ref[:, start + kind * width:start + (kind + 1) * width])
    qkv_ref[...] = jnp.concatenate(pieces, axis=1)[:SHARD]
    out_ref[...] = final_ref[:SHARD, :INNER]
    gain_ref[...] = final_ref[:, OUT_END - 128:OUT_END].T[GAIN_AT % 128:GAIN_AT % 128 + 1, :SHARD]


def on_device(patches, window_index, window_live, d_merged, w_qkv, w_out, merge_gain):
    vmem = pl.BlockSpec(memory_space=pltpu.VMEM)
    hbm = pl.BlockSpec(memory_space=pl.ANY)
    scratch = [
        pltpu.SMEM((1, SLOTS), jnp.int32),
        pltpu.VMEM((1, ROWS), jnp.int32),
        pltpu.VMEM((D,), F32),
        pltpu.VMEM((16, COLS), F32),
        pltpu.VMEM((ROWS, D), BF),
        pltpu.VMEM((ROWS // 4, 4 * D), BF),
        pltpu.VMEM((3 * INNER, D), BF),
        pltpu.VMEM((INNER, D), BF),
        pltpu.VMEM((D, ROWS), F32),
        pltpu.VMEM((D, ROWS), F32),
        pltpu.VMEM((ROWS, D), F32),
        pltpu.VMEM((ROWS, D), BF),
        pltpu.VMEM((3 * INNER, ROWS), BF),
        pltpu.VMEM((PAIRS, HEADS, WIN, 128), F32),
        pltpu.VMEM((ROWS, D), BF),
        pltpu.VMEM((INNER, ROWS), BF),
        pltpu.VMEM((2, 3, 2, HALF, ROWS), BF),
        pltpu.VMEM((COLS, ROWS), BF),
        pltpu.VMEM((2, HALF, 128), F32),
        pltpu.SemaphoreType.DMA((17,)),
    ]
    for first, width, route in PARTS:
        shape = second_shape(width)
        scratch += [
            pltpu.VMEM((4, BLOCK, width), BF),
            pltpu.VMEM((4, BLOCK, width), BF),
            pltpu.VMEM((2, 80, width), BF),
            pltpu.VMEM((2, BLOCK, width), BF),
            pltpu.VMEM((4,) + shape, BF),
            pltpu.VMEM((3,) + shape, BF),
            pltpu.VMEM((4, 16, width), BF),
            pltpu.VMEM((3, 16, width), BF),
        ]
    count = PER_PART * len(PARTS)
    scratch += [pltpu.SemaphoreType.DMA((count,)), pltpu.SemaphoreType.DMA((count,))]
    merged, final = pl.pallas_call(
        main_kernel,
        out_shape=(
            jax.ShapeDtypeStruct((ROWS // 4, 4 * D), BF),
            jax.ShapeDtypeStruct((16, COLS), F32),
        ),
        in_specs=[hbm] * 7,
        out_specs=(hbm, hbm),
        scratch_shapes=scratch,
        compiler_params=pltpu.CompilerParams(
            collective_id=0, has_side_effects=True, vmem_limit_bytes=62 * 2**20
        ),
        cost_estimate=pl.CostEstimate(
            flops=14_000_000_000, bytes_accessed=14_000_000, transcendentals=400_000
        ),
    )(window_live, window_index, merge_gain, patches, d_merged, w_qkv.T, w_out)
    merged, qkv, out, gain = pl.pallas_call(
        last_kernel,
        out_shape=(
            jax.ShapeDtypeStruct((ROWS // 4, 4 * D), BF),
            jax.ShapeDtypeStruct((SHARD, 3 * INNER), F32),
            jax.ShapeDtypeStruct((SHARD, INNER), F32),
            jax.ShapeDtypeStruct((1, SHARD), F32),
        ),
        in_specs=[vmem, vmem],
        out_specs=(vmem, vmem, vmem, vmem),
    )(final, merged)
    return merged, qkv, out.T, gain.reshape(SHARD)


def solution(mesh):
    both = ("dp", "vis")
    rows = P(both, None)
    return jax.shard_map(
        on_device,
        mesh=mesh,
        in_specs=(rows, rows, rows, rows, P(), P(), P()),
        out_specs=(rows, rows, P(None, both), P(both)),
        check_vma=False,
    )
```

```python
import functools

import jax
import jax.numpy as jnp
from jax import lax
from jax.experimental import pallas as pl
from jax.experimental.pallas import tpu as pltpu
from jax.sharding import PartitionSpec as P

D = 1280
HEADS = 12
HD = 80
INNER = HEADS * HD
WIN = 64
SLOTS = 8
ROWS = SLOTS * WIN
PAIRS = SLOTS // 2
EPSILON = 1e-06
NEGATIVE = -1e30
SCALE = HD ** (-0.5)
SHARD = 10
HALF = D // 2
BLOCK = HALF // 4
GROUPS = ((0, 1024), (1024, 2560), (2560, 3584), (3584, 4096))
GROUP_HEADS = ((0, 0), (0, 6), (6, 10), (10, 12))
GROUP_ENDS = tuple(end for _, end in GROUPS)
COLS = 4096
OUT_END = GROUPS[0][1]
GAIN_AT = INNER
MESH = pl.DeviceIdType.MESH
BF = jnp.bfloat16
F32 = jnp.float32

ROUTES = ("yxz", "xzy", "zyx")
PARTS = (
    (0, 256, 0), (256, 256, 1), (512, 512, 2),
    (1024, 512, 0), (1536, 512, 1), (2048, 512, 2),
    (2560, 256, 0), (2816, 512, 1), (3328, 256, 2),
    (3584, 256, 0), (3840, 256, 2),
)
PER_PART = 13
BUFFERS = 8


def mm(a, b):
    return lax.dot_general(a, b, (((1,), (0,)), ((), ())), preferred_element_type=F32)


def mm_nt(a, b):
    return lax.dot_general(a, b, (((1,), (1,)), ((), ())), preferred_element_type=F32)


def mm_tn(a, b):
    return lax.dot_general(a, b, (((0,), (0,)), ((), ())), preferred_element_type=F32)


def stack_pair(compact, left):
    zero = jnp.zeros_like(compact)
    return jnp.concatenate(
        [jnp.where(left, compact, zero), jnp.where(left, zero, compact)], axis=0
    ).astype(BF)


def folded(width):
    return width % 256 == 0


def second_shape(width):
    return (80, width // 2) if folded(width) else (48, width)


def joined_row(kind, head):
    for (start, _), (first, end) in zip(GROUPS, GROUP_HEADS):
        if first <= head < end:
            return start + (kind * (end - first) + head - first) * HD


def fine_row(route, first, second, third, core):
    at = dict(zip(ROUTES[route], (first, second, third)))
    return ((at["y"] * 4 + at["x"]) * 2 + core) * 40 + at["z"] * SHARD


def order_rows(left_ops, operand, tall, core, first):
    for b in range(0, 4, 2):
        to = first * BLOCK + b * 40
        pieces = []
        for c in (b, b + 1):
            at = fine_row(0, first, c, 0, core)
            pieces.append(tall[at:at + 40, :])
        left_ops[operand, 0, core, to:to + 80, :] = jnp.concatenate(pieces, axis=0).astype(BF)


def order_rows_fine(left_ops, operand, tall, tall_z, route, core, first):
    base = core * HALF + first * BLOCK
    for second in range(4):
        for third in range(4):
            to = base + second * 40 + third * SHARD
            at = fine_row(route, first, second, third, core)
            tall_z[to:to + SHARD, :] = tall[at:at + SHARD, :]
    left_ops[operand, route, core, first * BLOCK:(first + 1) * BLOCK] = tall_z[
        base:base + BLOCK, :
    ].astype(BF)


def main_kernel(
    live_hbm, index_hbm, gain_hbm, patches_hbm, cot_hbm, wqkv_hbm, wout_hbm,
    merged_hbm, final_hbm,
    live_ref, index_ref, gain_ref, final_ref,
    patches, wide_rows, wqkv, wout, tall, tall_z, att, rows_low, packed_t, probs, d_att, d_ctx_t,
    left_ops, right_op, gain_cols, local_sems, *scratch,
):
    sends, recvs = scratch[-2:]
    buffers = [scratch[BUFFERS * i:BUFFERS * (i + 1)] for i in range(len(PARTS))]
    loads = [
        pltpu.make_async_copy(src, dst, local_sems.at[i])
        for i, (src, dst) in enumerate(
            [(index_hbm, index_ref), (patches_hbm, patches), (live_hbm, live_ref), (gain_hbm, gain_ref)]
            + [(cot_hbm, wide_rows)]
            + [(wqkv_hbm.at[pl.ds(480 * n, 480)], wqkv.at[pl.ds(480 * n, 480)]) for n in range(6)]
            + [(wout_hbm, wout)]
        )
    ]
    for load in loads:
        load.start()

    dp = lax.axis_index("dp")
    core = dp % 2
    place = {"x": (dp // 2) % 4, "y": dp // 8, "z": lax.axis_index("vis")}

    def coordinate(at, side):
        return {"dp": (at["y"] * 4 + at["x"]) * 2 + side, "vis": at["z"]}

    pair_device = coordinate(place, 1 - core)
    near = {(axis, step): (place[axis] + step) % 4 for axis in "xyz" for step in (1, 2, 3)}
    devices = {key: coordinate({**place, key[0]: value}, core) for key, value in near.items()}
    barrier = pltpu.get_barrier_semaphore()
    for partner in [pair_device] + list(devices.values()):
        pl.semaphore_signal(barrier, inc=1, device_id=partner, device_id_type=MESH)

    started = {}
    stored = []

    def send(part, number, src, dst, target):
        copy = pltpu.make_async_remote_copy(
            src_ref=src, dst_ref=dst,
            send_sem=sends.at[PER_PART * part + number],
            recv_sem=recvs.at[PER_PART * part + number],
            device_id=target, device_id_type=MESH,
        )
        copy.start()
        started[part, number] = copy

    def arrived(part, number):
        started[part, number].wait_recv()

    def tiles(part):
        width = PARTS[part][1]
        return [(at, min(256, width - at)) for at in range(0, width, 256)]

    def product(part, side, at, size):
        first, width, route = PARTS[part]
        operand = 1 if first < OUT_END else 0
        out = mm_nt(left_ops[operand, route, side], right_op[first + at:first + at + size, :])
        if first + at + size == OUT_END:
            out = out + jnp.concatenate([jnp.zeros((HALF, size - 128), F32), gain_cols[side]], axis=1)
        return out

    def make_other(part):
        own, from_pair = buffers[part][:2]
        for at, size in tiles(part):
            value = product(part, 1 - core, at, size).astype(BF)
            for b in range(4):
                own[b, :, at:at + size] = value[BLOCK * b:BLOCK * (b + 1)]
        send(part, 0, own, from_pair, pair_device)

    def make_own(part):
        axis = ROUTES[PARTS[part][2]][0]
        own, from_pair, mid, wide = buffers[part][:4]
        started.pop((part, 0)).wait()
        for at, size in tiles(part):
            value = product(part, core, at, size)
            for b in range(4):
                own[b, :, at:at + size] = (
                    value[BLOCK * b:BLOCK * (b + 1)] + from_pair[b, :, at:at + size].astype(F32)
                ).astype(BF)
        up, far, down = (near[axis, step] for step in (1, 2, 3))
        low, high = pl.ds(0, 80), pl.ds(80, 80)
        send(part, 1, own.at[far, low], mid.at[0], devices[axis, 1])
        send(part, 2, own.at[far, high], mid.at[1], devices[axis, 3])
        send(part, 3, own.at[up, high], wide.at[0, high], devices[axis, 1])
        send(part, 4, own.at[down, low], wide.at[1, low], devices[axis, 3])

    def pass_on(part):
        axis = ROUTES[PARTS[part][2]][0]
        own, from_pair, mid, wide = buffers[part][:4]
        up, down = near[axis, 1], near[axis, 3]
        low, high = pl.ds(0, 80), pl.ds(80, 80)
        arrived(part, 1)
        own[up, low, :] = (own[up, low, :].astype(F32) + mid[0].astype(F32)).astype(BF)
        send(part, 5, own.at[up, low], wide.at[0, low], devices[axis, 1])
        arrived(part, 2)
        own[down, high, :] = (own[down, high, :].astype(F32) + mid[1].astype(F32)).astype(BF)
        send(part, 6, own.at[down, high], wide.at[1, high], devices[axis, 3])

    def second(part):
        first, width, route = PARTS[part]
        axis = ROUTES[route][1]
        own, from_pair, mid, wide, two, two_in = buffers[part][:6]
        for number in (3, 4, 5, 6):
            arrived(part, number)
        value = own[place[ROUTES[route][0]]].astype(F32) + wide[0].astype(F32) + wide[1].astype(F32)
        if folded(width):
            for b in range(4):
                rows = value[40 * b:40 * (b + 1)]
                two[b] = jnp.concatenate(
                    [rows[:, :width // 2], rows[:, width // 2:]], axis=0
                ).astype(BF)
        else:
            value = jnp.concatenate([value, jnp.zeros((8, width), F32)], axis=0)
            for b in range(4):
                two[b] = value[40 * b:40 * b + 48].astype(BF)
        for step in (1, 2, 3):
            send(part, 6 + step, two.at[near[axis, step]], two_in.at[step - 1], devices[axis, step])

    def third(part):
        first, width, route = PARTS[part]
        axis = ROUTES[route][2]
        two, two_in, three, three_in = buffers[part][4:8]
        value = two[place[ROUTES[route][1]]].astype(F32)
        for step in (1, 2, 3):
            arrived(part, 6 + step)
            value = value + two_in[step - 1].astype(F32)
        if folded(width):
            value = jnp.concatenate([value[:40], value[40:]], axis=1)
            value = jnp.concatenate([value, jnp.zeros((8, width), F32)], axis=0)
        for b in range(4):
            three[b] = value[SHARD * b:SHARD * b + 16].astype(BF)
        for step in (1, 2, 3):
            send(part, 9 + step, three.at[near[axis, step]], three_in.at[step - 1], devices[axis, step])

    def finish(part):
        first, width, route = PARTS[part]
        three, three_in = buffers[part][6:8]
        value = three[place[ROUTES[route][2]]].astype(F32)
        for step in (1, 2, 3):
            arrived(part, 9 + step)
            value = value + three_in[step - 1].astype(F32)
        final_ref[:, first:first + width] = value
        if first + width in GROUP_ENDS:
            group = GROUP_ENDS.index(first + width)
            cols = pl.ds(GROUPS[group][0], first + width - GROUPS[group][0])
            copy = pltpu.make_async_copy(
                final_ref.at[:, cols], final_hbm.at[:, cols], local_sems.at[13 + group]
            )
            copy.start()
            stored.append(copy)

    loads[0].wait()
    pick_t = (lax.broadcasted_iota(jnp.int32, (ROWS, ROWS), 0) == index_ref[...]).astype(BF)
    pick = pick_t.T
    loads[1].wait()
    for n in range(5):
        cols = slice(256 * n, 256 * (n + 1))
        att[:, cols] = mm(pick, patches[:, cols])
    row_i = lax.broadcasted_iota(jnp.int32, (ROWS, ROWS), 0)
    col_i = lax.broadcasted_iota(jnp.int32, (ROWS, ROWS), 1)
    spread = (row_i == (col_i % 128) * 4 + col_i // 128).astype(BF)
    loads[4].wait()
    for n in range(5):
        cols = slice(256 * n, 256 * (n + 1))
        cot = jnp.concatenate(
            [wide_rows[:, j * D + 256 * n:j * D + 256 * (n + 1)] for j in range(4)], axis=0
        )
        d_att[:, cols] = mm(spread, cot).astype(BF)
    for n in range(SLOTS):
        rows = slice(WIN * n, WIN * (n + 1))
        picked = att[rows, :]
        normed = picked * lax.rsqrt(jnp.mean(picked * picked, -1, keepdims=True) + EPSILON)
        rows_low[rows, :] = normed.astype(BF)
    for (start, end), (first, last) in zip(GROUPS, GROUP_HEADS):
        used = start + (3 * HD * (last - first) or INNER)
        right_op[used:end, :] = jnp.zeros((end - used, ROWS), BF)

    def turn(source, n):
        cols = slice(256 * n, 256 * (n + 1))
        tall[cols, :] = source[:, cols].astype(F32).T

    corners = [(core, first) for core in range(2) for first in range(4)]
    beside = [functools.partial(turn, rows_low, n) for n in range(5)]
    beside += [functools.partial(order_rows, left_ops, 0, tall, *corner) for corner in corners]
    for route in (1, 2):
        beside += [
            functools.partial(order_rows_fine, left_ops, 0, tall, tall_z, route, *corner)
            for corner in corners
        ]
    for n in range(6):
        rows = slice(480 * n, 480 * (n + 1))
        loads[5 + n].wait()
        packed_t[rows, :] = mm_nt(wqkv[rows, :], rows_low[...]).astype(BF)
        for piece in beside[5 * n:5 * n + 5]:
            piece()

    loads[2].wait()
    loads[3].wait()
    left = lax.broadcasted_iota(jnp.int32, (WIN, 128), 1) < WIN
    key_row = lax.broadcasted_iota(jnp.int32, (WIN, 128), 0)
    masks = [
        key_row < jnp.where(left, live_ref[0, 2 * pair], live_ref[0, 2 * pair + 1])
        for pair in range(PAIRS)
    ]

    def head_rows(kind, h):
        start = kind * INNER + HD * h
        return slice(start, start + HD) if isinstance(h, int) else pl.ds(pl.multiple_of(start, 16), HD)

    def forward(step, carry):
        todo = [
            (step * 3 + i, pair, slice(128 * pair, 128 * (pair + 1)))
            for i in range(3) for pair in range(PAIRS)
        ]
        fulls = [mm_tn(packed_t[head_rows(1, h), c], packed_t[head_rows(0, h), c]) for h, pair, c in todo]
        stacks = []
        for (h, pair, c), full in zip(todo, fulls):
            scores = jnp.where(left, full[:WIN], full[WIN:]) * SCALE
            scores = jnp.where(masks[pair], scores, NEGATIVE)
            top = jnp.max(scores, axis=0, keepdims=True)
            weight = jnp.exp(scores - top)
            prob = weight * (1.0 / jnp.sum(weight, axis=0, keepdims=True))
            probs[pair, h] = prob
            stacks.append(stack_pair(prob, left))
        for (h, pair, c), stack in zip(todo, stacks):
            right_op[head_rows(0, h), c] = mm(packed_t[head_rows(2, h), c], stack).astype(BF)
        return carry

    lax.fori_loop(0, HEADS // 3, forward, 0)

    loads[11].wait()
    ctx = right_op[:INNER, :].T
    for n in range(5):
        cols = slice(256 * n, 256 * (n + 1))
        att[:, cols] += mm(ctx, wout[:, cols])
    gain = gain_ref[...].reshape(1, D)

    def norm_block(block, total):
        rows = pl.ds(pl.multiple_of(block * WIN, WIN), WIN)
        alive = (
            lax.broadcasted_iota(jnp.int32, (WIN, 1), 0) < live_ref[0, block]
        ).astype(F32)
        attended = att[rows, :]
        inv = lax.rsqrt(jnp.mean(attended * attended, -1, keepdims=True) + EPSILON)
        normalized = attended * inv
        patches[rows, :] = (normalized * gain * alive).astype(BF)
        grad_rows = d_att[rows, :].astype(F32) * alive
        prod = grad_rows * normalized
        scaled = grad_rows * gain
        mean = jnp.mean(scaled * normalized, -1, keepdims=True)
        d_att[rows, :] = (inv * (scaled - normalized * mean)).astype(BF)
        return total + jnp.sum(prod, axis=0, keepdims=True)

    total = lax.fori_loop(0, SLOTS, norm_block, jnp.zeros((1, D), F32))
    for n in range(5):
        turn(d_att, n)
    for corner in corners:
        order_rows(left_ops, 1, tall, *corner)
    pl.semaphore_wait(barrier, 1 + len(devices))
    make_other(0)
    for corner in corners:
        order_rows_fine(left_ops, 1, tall, tall_z, 1, *corner)
    make_other(1)
    for corner in corners:
        order_rows_fine(left_ops, 1, tall, tall_z, 2, *corner)
    tall[:, :128] = jnp.broadcast_to(total, (128, D)).T
    lane = lax.broadcasted_iota(jnp.int32, (SHARD, 128), 1)
    for side in range(2):
        for first in range(4):
            for second_place in range(4):
                for third_place in range(4):
                    to = first * BLOCK + second_place * 40 + third_place * SHARD
                    at = fine_row(2, first, second_place, third_place, side)
                    gain_cols[side, to:to + SHARD, :] = jnp.where(
                        lane >= GAIN_AT % 128, tall[at:at + SHARD, :128], 0.0
                    )
    make_other(2)
    for n in range(3):
        rows = slice(320 * n, 320 * (n + 1))
        d_ctx_t[rows, :] = mm_nt(wout[rows, :], d_att[...]).astype(BF)
    def backward(heads):
        todo = [
            (h, pair, slice(128 * pair, 128 * (pair + 1))) for h in heads for pair in range(PAIRS)
        ]
        dcs = [d_ctx_t[head_rows(0, h), c] for h, pair, c in todo]
        fulls = [mm_tn(packed_t[head_rows(2, h), c], dc) for (h, pair, c), dc in zip(todo, dcs)]
        stacks = []
        for (h, pair, c), full in zip(todo, fulls):
            prob = probs[pair, h]
            d_prob = jnp.where(left, full[:WIN], full[WIN:])
            dot = jnp.sum(d_prob * prob, axis=0, keepdims=True)
            stacks.append(stack_pair(prob * (d_prob - dot) * SCALE, left))
        for (h, pair, c), dc in zip(todo, dcs):
            to = joined_row(2, h)
            right_op[to:to + HD, c] = mm_nt(dc, stack_pair(probs[pair, h], left)).astype(BF)
        for (h, pair, c), stack in zip(todo, stacks):
            to = joined_row(0, h)
            right_op[to:to + HD, c] = mm(packed_t[head_rows(1, h), c], stack).astype(BF)
            to = joined_row(1, h)
            right_op[to:to + HD, c] = mm_nt(packed_t[head_rows(0, h), c], stack).astype(BF)

    def each(step, group):
        start, end = GROUPS[group]
        for part, (first, width, route) in enumerate(PARTS):
            if start <= first < end:
                step(part)

    each(make_own, 0)
    backward(range(0, 6))
    each(make_other, 1)
    backward(range(6, 10))
    each(make_own, 1)
    each(make_other, 2)
    backward(range(10, 12))
    each(pass_on, 0)
    each(make_own, 2)
    each(make_other, 3)
    gather = (col_i == (row_i % 128) * 4 + row_i // 128).astype(BF)
    for n in range(5):
        back = mm(gather, patches[:, 256 * n:256 * (n + 1)]).astype(BF)
        for j in range(4):
            wide_rows[:, j * D + 256 * n:j * D + 256 * (n + 1)] = back[128 * j:128 * (j + 1)]
    store = pltpu.make_async_copy(wide_rows, merged_hbm, local_sems.at[12])
    store.start()

    each(make_own, 3)
    each(second, 0)
    for group in (1, 2, 3):
        each(pass_on, group)
    each(third, 0)
    for group in (1, 2, 3):
        each(second, group)
    each(finish, 0)
    for step in (third, finish):
        for group in (1, 2, 3):
            each(step, group)
    for copy in started.values():
        copy.wait_send()
    for copy in stored + [store]:
        copy.wait()


def last_kernel(final_ref, merged_in, merged_ref, qkv_ref, out_ref, gain_ref):
    merged_ref[...] = merged_in[...]
    pieces = []
    for kind in range(3):
        for (start, _), (first, end) in zip(GROUPS[1:], GROUP_HEADS[1:]):
            width = HD * (end - first)
            pieces.append(final_ref[:, start + kind * width:start + (kind + 1) * width])
    qkv_ref[...] = jnp.concatenate(pieces, axis=1)[:SHARD]
    out_ref[...] = final_ref[:SHARD, :INNER]
    gain_ref[...] = final_ref[:, OUT_END - 128:OUT_END].T[GAIN_AT % 128:GAIN_AT % 128 + 1, :SHARD]


def on_device(patches, window_index, window_live, d_merged, w_qkv, w_out, merge_gain):
    vmem = pl.BlockSpec(memory_space=pltpu.VMEM)
    hbm = pl.BlockSpec(memory_space=pl.ANY)
    scratch = [
        pltpu.SMEM((1, SLOTS), jnp.int32),
        pltpu.VMEM((1, ROWS), jnp.int32),
        pltpu.VMEM((D,), F32),
        pltpu.VMEM((16, COLS), F32),
        pltpu.VMEM((ROWS, D), BF),
        pltpu.VMEM((ROWS // 4, 4 * D), BF),
        pltpu.VMEM((3 * INNER, D), BF),
        pltpu.VMEM((INNER, D), BF),
        pltpu.VMEM((D, ROWS), F32),
        pltpu.VMEM((D, ROWS), F32),
        pltpu.VMEM((ROWS, D), F32),
        pltpu.VMEM((ROWS, D), BF),
        pltpu.VMEM((3 * INNER, ROWS), BF),
        pltpu.VMEM((PAIRS, HEADS, WIN, 128), F32),
        pltpu.VMEM((ROWS, D), BF),
        pltpu.VMEM((INNER, ROWS), BF),
        pltpu.VMEM((2, 3, 2, HALF, ROWS), BF),
        pltpu.VMEM((COLS, ROWS), BF),
        pltpu.VMEM((2, HALF, 128), F32),
        pltpu.SemaphoreType.DMA((17,)),
    ]
    for first, width, route in PARTS:
        shape = second_shape(width)
        scratch += [
            pltpu.VMEM((4, BLOCK, width), BF),
            pltpu.VMEM((4, BLOCK, width), BF),
            pltpu.VMEM((2, 80, width), BF),
            pltpu.VMEM((2, BLOCK, width), BF),
            pltpu.VMEM((4,) + shape, BF),
            pltpu.VMEM((3,) + shape, BF),
            pltpu.VMEM((4, 16, width), BF),
            pltpu.VMEM((3, 16, width), BF),
        ]
    count = PER_PART * len(PARTS)
    scratch += [pltpu.SemaphoreType.DMA((count,)), pltpu.SemaphoreType.DMA((count,))]
    merged, final = pl.pallas_call(
        main_kernel,
        out_shape=(
            jax.ShapeDtypeStruct((ROWS // 4, 4 * D), BF),
            jax.ShapeDtypeStruct((16, COLS), F32),
        ),
        in_specs=[hbm] * 7,
        out_specs=(hbm, hbm),
        scratch_shapes=scratch,
        compiler_params=pltpu.CompilerParams(
            collective_id=0, has_side_effects=True, vmem_limit_bytes=62 * 2**20
        ),
        cost_estimate=pl.CostEstimate(
            flops=14_000_000_000, bytes_accessed=14_000_000, transcendentals=400_000
        ),
    )(window_live, window_index, merge_gain, patches, d_merged, w_qkv.T, w_out)
    merged, qkv, out, gain = pl.pallas_call(
        last_kernel,
        out_shape=(
            jax.ShapeDtypeStruct((ROWS // 4, 4 * D), BF),
            jax.ShapeDtypeStruct((SHARD, 3 * INNER), F32),
            jax.ShapeDtypeStruct((SHARD, INNER), F32),
            jax.ShapeDtypeStruct((1, SHARD), F32),
        ),
        in_specs=[vmem, vmem],
        out_specs=(vmem, vmem, vmem, vmem),
    )(final, merged)
    return merged, qkv, out.T, gain.reshape(SHARD)


def solution(mesh):
    both = ("dp", "vis")
    rows = P(both, None)
    return jax.shard_map(
        on_device,
        mesh=mesh,
        in_specs=(rows, rows, rows, rows, P(), P(), P()),
        out_specs=(rows, rows, P(None, both), P(both)),
        check_vma=False,
    )
```

```python
import functools

import jax
import jax.numpy as jnp
from jax import lax
from jax.experimental import pallas as pl
from jax.experimental.pallas import tpu as pltpu
from jax.sharding import PartitionSpec as P

D = 1280
HEADS = 12
HD = 80
INNER = HEADS * HD
WIN = 64
SLOTS = 8
ROWS = SLOTS * WIN
PAIRS = SLOTS // 2
EPSILON = 1e-06
NEGATIVE = -1e30
SCALE = HD ** (-0.5)
SHARD = 10
HALF = D // 2
BLOCK = HALF // 4
GROUPS = ((0, 1024), (1024, 2560), (2560, 3584), (3584, 4096))
GROUP_HEADS = ((0, 0), (0, 6), (6, 10), (10, 12))
GROUP_ENDS = tuple(end for _, end in GROUPS)
COLS = 4096
OUT_END = GROUPS[0][1]
GAIN_AT = INNER
MESH = pl.DeviceIdType.MESH
BF = jnp.bfloat16
F32 = jnp.float32

ROUTES = ("yxz", "xzy", "zyx")
PARTS = (
    (0, 256, 0), (256, 256, 1), (512, 512, 2),
    (1024, 512, 0), (1536, 512, 1), (2048, 512, 2),
    (2560, 256, 0), (2816, 512, 1), (3328, 256, 2),
    (3584, 256, 0), (3840, 256, 2),
)
PER_PART = 13
BUFFERS = 8


def mm(a, b):
    return lax.dot_general(a, b, (((1,), (0,)), ((), ())), preferred_element_type=F32)


def mm_nt(a, b):
    return lax.dot_general(a, b, (((1,), (1,)), ((), ())), preferred_element_type=F32)


def mm_tn(a, b):
    return lax.dot_general(a, b, (((0,), (0,)), ((), ())), preferred_element_type=F32)


def stack_pair(compact, left):
    zero = jnp.zeros_like(compact)
    return jnp.concatenate(
        [jnp.where(left, compact, zero), jnp.where(left, zero, compact)], axis=0
    ).astype(BF)


def folded(width):
    return width % 256 == 0


def second_shape(width):
    return (80, width // 2) if folded(width) else (48, width)


def joined_row(kind, head):
    for (start, _), (first, end) in zip(GROUPS, GROUP_HEADS):
        if first <= head < end:
            return start + (kind * (end - first) + head - first) * HD


def fine_row(route, first, second, third, core):
    at = dict(zip(ROUTES[route], (first, second, third)))
    return ((at["y"] * 4 + at["x"]) * 2 + core) * 40 + at["z"] * SHARD


def order_rows(left_ops, operand, tall, core, first):
    for b in range(0, 4, 2):
        to = first * BLOCK + b * 40
        pieces = []
        for c in (b, b + 1):
            at = fine_row(0, first, c, 0, core)
            pieces.append(tall[at:at + 40, :])
        left_ops[operand, 0, core, to:to + 80, :] = jnp.concatenate(pieces, axis=0).astype(BF)


def order_rows_fine(left_ops, operand, tall, tall_z, route, core, first):
    base = core * HALF + first * BLOCK
    for second in range(4):
        for third in range(4):
            to = base + second * 40 + third * SHARD
            at = fine_row(route, first, second, third, core)
            tall_z[to:to + SHARD, :] = tall[at:at + SHARD, :]
    left_ops[operand, route, core, first * BLOCK:(first + 1) * BLOCK] = tall_z[
        base:base + BLOCK, :
    ].astype(BF)


def main_kernel(
    live_hbm, index_hbm, gain_hbm, patches_hbm, cot_hbm, wqkv_hbm, wout_hbm,
    merged_hbm, final_hbm,
    live_ref, index_ref, gain_ref, final_ref,
    patches, wide_rows, wqkv, wout, tall, tall_z, att, rows_low, packed_t, probs, d_att, d_ctx_t,
    left_ops, right_op, gain_cols, local_sems, *scratch,
):
    sends, recvs = scratch[-2:]
    buffers = [scratch[BUFFERS * i:BUFFERS * (i + 1)] for i in range(len(PARTS))]
    loads = [
        pltpu.make_async_copy(src, dst, local_sems.at[i])
        for i, (src, dst) in enumerate(
            [(index_hbm, index_ref), (patches_hbm, patches), (live_hbm, live_ref), (gain_hbm, gain_ref)]
            + [(cot_hbm, wide_rows)]
            + [(wqkv_hbm.at[pl.ds(480 * n, 480)], wqkv.at[pl.ds(480 * n, 480)]) for n in range(6)]
            + [(wout_hbm, wout)]
        )
    ]
    for load in loads:
        load.start()

    dp = lax.axis_index("dp")
    core = dp % 2
    place = {"x": (dp // 2) % 4, "y": dp // 8, "z": lax.axis_index("vis")}

    def coordinate(at, side):
        return {"dp": (at["y"] * 4 + at["x"]) * 2 + side, "vis": at["z"]}

    pair_device = coordinate(place, 1 - core)
    near = {(axis, step): (place[axis] + step) % 4 for axis in "xyz" for step in (1, 2, 3)}
    devices = {key: coordinate({**place, key[0]: value}, core) for key, value in near.items()}
    barrier = pltpu.get_barrier_semaphore()
    for partner in [pair_device] + list(devices.values()):
        pl.semaphore_signal(barrier, inc=1, device_id=partner, device_id_type=MESH)

    started = {}
    stored = []

    def send(part, number, src, dst, target):
        copy = pltpu.make_async_remote_copy(
            src_ref=src, dst_ref=dst,
            send_sem=sends.at[PER_PART * part + number],
            recv_sem=recvs.at[PER_PART * part + number],
            device_id=target, device_id_type=MESH,
        )
        copy.start()
        started[part, number] = copy

    def arrived(part, number):
        started[part, number].wait_recv()

    def tiles(part):
        width = PARTS[part][1]
        return [(at, min(256, width - at)) for at in range(0, width, 256)]

    def product(part, side, at, size):
        first, width, route = PARTS[part]
        operand = 1 if first < OUT_END else 0
        out = mm_nt(left_ops[operand, route, side], right_op[first + at:first + at + size, :])
        if first + at + size == OUT_END:
            out = out + jnp.concatenate([jnp.zeros((HALF, size - 128), F32), gain_cols[side]], axis=1)
        return out

    def make_other(part):
        own, from_pair = buffers[part][:2]
        for at, size in tiles(part):
            value = product(part, 1 - core, at, size).astype(BF)
            for b in range(4):
                own[b, :, at:at + size] = value[BLOCK * b:BLOCK * (b + 1)]
        send(part, 0, own, from_pair, pair_device)

    def make_own(part):
        axis = ROUTES[PARTS[part][2]][0]
        own, from_pair, mid, wide = buffers[part][:4]
        started.pop((part, 0)).wait()
        for at, size in tiles(part):
            value = product(part, core, at, size)
            for b in range(4):
                own[b, :, at:at + size] = (
                    value[BLOCK * b:BLOCK * (b + 1)] + from_pair[b, :, at:at + size].astype(F32)
                ).astype(BF)
        up, far, down = (near[axis, step] for step in (1, 2, 3))
        low, high = pl.ds(0, 80), pl.ds(80, 80)
        send(part, 1, own.at[far, low], mid.at[0], devices[axis, 1])
        send(part, 2, own.at[far, high], mid.at[1], devices[axis, 3])
        send(part, 3, own.at[up, high], wide.at[0, high], devices[axis, 1])
        send(part, 4, own.at[down, low], wide.at[1, low], devices[axis, 3])

    def pass_on(part):
        axis = ROUTES[PARTS[part][2]][0]
        own, from_pair, mid, wide = buffers[part][:4]
        up, down = near[axis, 1], near[axis, 3]
        low, high = pl.ds(0, 80), pl.ds(80, 80)
        arrived(part, 1)
        own[up, low, :] = (own[up, low, :].astype(F32) + mid[0].astype(F32)).astype(BF)
        send(part, 5, own.at[up, low], wide.at[0, low], devices[axis, 1])
        arrived(part, 2)
        own[down, high, :] = (own[down, high, :].astype(F32) + mid[1].astype(F32)).astype(BF)
        send(part, 6, own.at[down, high], wide.at[1, high], devices[axis, 3])

    def second(part):
        first, width, route = PARTS[part]
        axis = ROUTES[route][1]
        own, from_pair, mid, wide, two, two_in = buffers[part][:6]
        for number in (3, 4, 5, 6):
            arrived(part, number)
        value = own[place[ROUTES[route][0]]].astype(F32) + wide[0].astype(F32) + wide[1].astype(F32)
        if folded(width):
            for b in range(4):
                rows = value[40 * b:40 * (b + 1)]
                two[b] = jnp.concatenate(
                    [rows[:, :width // 2], rows[:, width // 2:]], axis=0
                ).astype(BF)
        else:
            value = jnp.concatenate([value, jnp.zeros((8, width), F32)], axis=0)
            for b in range(4):
                two[b] = value[40 * b:40 * b + 48].astype(BF)
        for step in (1, 2, 3):
            send(part, 6 + step, two.at[near[axis, step]], two_in.at[step - 1], devices[axis, step])

    def third(part):
        first, width, route = PARTS[part]
        axis = ROUTES[route][2]
        two, two_in, three, three_in = buffers[part][4:8]
        value = two[place[ROUTES[route][1]]].astype(F32)
        for step in (1, 2, 3):
            arrived(part, 6 + step)
            value = value + two_in[step - 1].astype(F32)
        if folded(width):
            value = jnp.concatenate([value[:40], value[40:]], axis=1)
            value = jnp.concatenate([value, jnp.zeros((8, width), F32)], axis=0)
        for b in range(4):
            three[b] = value[SHARD * b:SHARD * b + 16].astype(BF)
        for step in (1, 2, 3):
            send(part, 9 + step, three.at[near[axis, step]], three_in.at[step - 1], devices[axis, step])

    def finish(part):
        first, width, route = PARTS[part]
        three, three_in = buffers[part][6:8]
        value = three[place[ROUTES[route][2]]].astype(F32)
        for step in (1, 2, 3):
            arrived(part, 9 + step)
            value = value + three_in[step - 1].astype(F32)
        final_ref[:, first:first + width] = value
        if first + width in GROUP_ENDS:
            group = GROUP_ENDS.index(first + width)
            cols = pl.ds(GROUPS[group][0], first + width - GROUPS[group][0])
            copy = pltpu.make_async_copy(
                final_ref.at[:, cols], final_hbm.at[:, cols], local_sems.at[13 + group]
            )
            copy.start()
            stored.append(copy)

    loads[0].wait()
    pick_t = (lax.broadcasted_iota(jnp.int32, (ROWS, ROWS), 0) == index_ref[...]).astype(BF)
    pick = pick_t.T
    loads[1].wait()
    for n in range(5):
        cols = slice(256 * n, 256 * (n + 1))
        att[:, cols] = mm(pick, patches[:, cols])
    row_i = lax.broadcasted_iota(jnp.int32, (ROWS, ROWS), 0)
    col_i = lax.broadcasted_iota(jnp.int32, (ROWS, ROWS), 1)
    spread = (row_i == (col_i % 128) * 4 + col_i // 128).astype(BF)
    loads[4].wait()
    for n in range(5):
        cols = slice(256 * n, 256 * (n + 1))
        cot = jnp.concatenate(
            [wide_rows[:, j * D + 256 * n:j * D + 256 * (n + 1)] for j in range(4)], axis=0
        )
        d_att[:, cols] = mm(spread, cot).astype(BF)
    for n in range(SLOTS):
        rows = slice(WIN * n, WIN * (n + 1))
        picked = att[rows, :]
        normed = picked * lax.rsqrt(jnp.mean(picked * picked, -1, keepdims=True) + EPSILON)
        rows_low[rows, :] = normed.astype(BF)
    for (start, end), (first, last) in zip(GROUPS, GROUP_HEADS):
        used = start + (3 * HD * (last - first) or INNER)
        right_op[used:end, :] = jnp.zeros((end - used, ROWS), BF)

    def turn(source, n):
        cols = slice(256 * n, 256 * (n + 1))
        tall[cols, :] = source[:, cols].astype(F32).T

    corners = [(core, first) for core in range(2) for first in range(4)]
    beside = [functools.partial(turn, rows_low, n) for n in range(5)]
    beside += [functools.partial(order_rows, left_ops, 0, tall, *corner) for corner in corners]
    for route in (1, 2):
        beside += [
            functools.partial(order_rows_fine, left_ops, 0, tall, tall_z, route, *corner)
            for corner in corners
        ]
    for n in range(6):
        rows = slice(480 * n, 480 * (n + 1))
        loads[5 + n].wait()
        packed_t[rows, :] = mm_nt(wqkv[rows, :], rows_low[...]).astype(BF)
        for piece in beside[5 * n:5 * n + 5]:
            piece()

    loads[2].wait()
    loads[3].wait()
    left = lax.broadcasted_iota(jnp.int32, (WIN, 128), 1) < WIN
    key_row = lax.broadcasted_iota(jnp.int32, (WIN, 128), 0)
    masks = [
        key_row < jnp.where(left, live_ref[0, 2 * pair], live_ref[0, 2 * pair + 1])
        for pair in range(PAIRS)
    ]

    def head_rows(kind, h):
        start = kind * INNER + HD * h
        return slice(start, start + HD) if isinstance(h, int) else pl.ds(pl.multiple_of(start, 16), HD)

    def forward(step, carry):
        todo = [
            (step * 3 + i, pair, slice(128 * pair, 128 * (pair + 1)))
            for i in range(3) for pair in range(PAIRS)
        ]
        fulls = [mm_tn(packed_t[head_rows(1, h), c], packed_t[head_rows(0, h), c]) for h, pair, c in todo]
        stacks = []
        for (h, pair, c), full in zip(todo, fulls):
            scores = jnp.where(left, full[:WIN], full[WIN:]) * SCALE
            scores = jnp.where(masks[pair], scores, NEGATIVE)
            top = jnp.max(scores, axis=0, keepdims=True)
            weight = jnp.exp(scores - top)
            prob = weight * (1.0 / jnp.sum(weight, axis=0, keepdims=True))
            probs[pair, h] = prob
            stacks.append(stack_pair(prob, left))
        for (h, pair, c), stack in zip(todo, stacks):
            right_op[head_rows(0, h), c] = mm(packed_t[head_rows(2, h), c], stack).astype(BF)
        return carry

    lax.fori_loop(0, HEADS // 3, forward, 0)

    loads[11].wait()
    ctx = right_op[:INNER, :].T
    for n in range(5):
        cols = slice(256 * n, 256 * (n + 1))
        att[:, cols] += mm(ctx, wout[:, cols])
    gain = gain_ref[...].reshape(1, D)

    def norm_block(block, total):
        rows = pl.ds(pl.multiple_of(block * WIN, WIN), WIN)
        alive = (
            lax.broadcasted_iota(jnp.int32, (WIN, 1), 0) < live_ref[0, block]
        ).astype(F32)
        attended = att[rows, :]
        inv = lax.rsqrt(jnp.mean(attended * attended, -1, keepdims=True) + EPSILON)
        normalized = attended * inv
        patches[rows, :] = (normalized * gain * alive).astype(BF)
        grad_rows = d_att[rows, :].astype(F32) * alive
        prod = grad_rows * normalized
        scaled = grad_rows * gain
        mean = jnp.mean(scaled * normalized, -1, keepdims=True)
        d_att[rows, :] = (inv * (scaled - normalized * mean)).astype(BF)
        return total + jnp.sum(prod, axis=0, keepdims=True)

    total = lax.fori_loop(0, SLOTS, norm_block, jnp.zeros((1, D), F32))
    for n in range(5):
        turn(d_att, n)
    for corner in corners:
        order_rows(left_ops, 1, tall, *corner)
    pl.semaphore_wait(barrier, 1 + len(devices))
    make_other(0)
    for corner in corners:
        order_rows_fine(left_ops, 1, tall, tall_z, 1, *corner)
    make_other(1)
    for corner in corners:
        order_rows_fine(left_ops, 1, tall, tall_z, 2, *corner)
    tall[:, :128] = jnp.broadcast_to(total, (128, D)).T
    lane = lax.broadcasted_iota(jnp.int32, (SHARD, 128), 1)
    for side in range(2):
        for first in range(4):
            for second_place in range(4):
                for third_place in range(4):
                    to = first * BLOCK + second_place * 40 + third_place * SHARD
                    at = fine_row(2, first, second_place, third_place, side)
                    gain_cols[side, to:to + SHARD, :] = jnp.where(
                        lane >= GAIN_AT % 128, tall[at:at + SHARD, :128], 0.0
                    )
    make_other(2)
    for n in range(3):
        rows = slice(320 * n, 320 * (n + 1))
        d_ctx_t[rows, :] = mm_nt(wout[rows, :], d_att[...]).astype(BF)
    def backward(heads):
        todo = [
            (h, pair, slice(128 * pair, 128 * (pair + 1))) for h in heads for pair in range(PAIRS)
        ]
        dcs = [d_ctx_t[head_rows(0, h), c] for h, pair, c in todo]
        fulls = [mm_tn(packed_t[head_rows(2, h), c], dc) for (h, pair, c), dc in zip(todo, dcs)]
        stacks = []
        for (h, pair, c), full in zip(todo, fulls):
            prob = probs[pair, h]
            d_prob = jnp.where(left, full[:WIN], full[WIN:])
            dot = jnp.sum(d_prob * prob, axis=0, keepdims=True)
            stacks.append(stack_pair(prob * (d_prob - dot) * SCALE, left))
        for (h, pair, c), dc in zip(todo, dcs):
            to = joined_row(2, h)
            right_op[to:to + HD, c] = mm_nt(dc, stack_pair(probs[pair, h], left)).astype(BF)
        for (h, pair, c), stack in zip(todo, stacks):
            to = joined_row(0, h)
            right_op[to:to + HD, c] = mm(packed_t[head_rows(1, h), c], stack).astype(BF)
            to = joined_row(1, h)
            right_op[to:to + HD, c] = mm_nt(packed_t[head_rows(0, h), c], stack).astype(BF)

    def each(step, group):
        start, end = GROUPS[group]
        for part, (first, width, route) in enumerate(PARTS):
            if start <= first < end:
                step(part)

    each(make_own, 0)
    backward(range(0, 6))
    each(make_other, 1)
    backward(range(6, 10))
    each(make_own, 1)
    each(make_other, 2)
    backward(range(10, 12))
    each(pass_on, 0)
    each(make_own, 2)
    each(make_other, 3)
    each(make_own, 3)
    gather = (col_i == (row_i % 128) * 4 + row_i // 128).astype(BF)
    for n in range(5):
        back = mm(gather, patches[:, 256 * n:256 * (n + 1)]).astype(BF)
        for j in range(4):
            wide_rows[:, j * D + 256 * n:j * D + 256 * (n + 1)] = back[128 * j:128 * (j + 1)]
    store = pltpu.make_async_copy(wide_rows, merged_hbm, local_sems.at[12])
    store.start()

    each(second, 0)
    for group in (1, 2, 3):
        each(pass_on, group)
    each(third, 0)
    for group in (1, 2, 3):
        each(second, group)
    each(finish, 0)
    for step in (third, finish):
        for group in (1, 2, 3):
            each(step, group)
    for copy in started.values():
        copy.wait_send()
    for copy in stored + [store]:
        copy.wait()


def last_kernel(final_ref, merged_in, merged_ref, qkv_ref, out_ref, gain_ref):
    merged_ref[...] = merged_in[...]
    pieces = []
    for kind in range(3):
        for (start, _), (first, end) in zip(GROUPS[1:], GROUP_HEADS[1:]):
            width = HD * (end - first)
            pieces.append(final_ref[:, start + kind * width:start + (kind + 1) * width])
    qkv_ref[...] = jnp.concatenate(pieces, axis=1)[:SHARD]
    out_ref[...] = final_ref[:SHARD, :INNER]
    gain_ref[...] = final_ref[:, OUT_END - 128:OUT_END].T[GAIN_AT % 128:GAIN_AT % 128 + 1, :SHARD]


def on_device(patches, window_index, window_live, d_merged, w_qkv, w_out, merge_gain):
    vmem = pl.BlockSpec(memory_space=pltpu.VMEM)
    hbm = pl.BlockSpec(memory_space=pl.ANY)
    scratch = [
        pltpu.SMEM((1, SLOTS), jnp.int32),
        pltpu.VMEM((1, ROWS), jnp.int32),
        pltpu.VMEM((D,), F32),
        pltpu.VMEM((16, COLS), F32),
        pltpu.VMEM((ROWS, D), BF),
        pltpu.VMEM((ROWS // 4, 4 * D), BF),
        pltpu.VMEM((3 * INNER, D), BF),
        pltpu.VMEM((INNER, D), BF),
        pltpu.VMEM((D, ROWS), F32),
        pltpu.VMEM((D, ROWS), F32),
        pltpu.VMEM((ROWS, D), F32),
        pltpu.VMEM((ROWS, D), BF),
        pltpu.VMEM((3 * INNER, ROWS), BF),
        pltpu.VMEM((PAIRS, HEADS, WIN, 128), F32),
        pltpu.VMEM((ROWS, D), BF),
        pltpu.VMEM((INNER, ROWS), BF),
        pltpu.VMEM((2, 3, 2, HALF, ROWS), BF),
        pltpu.VMEM((COLS, ROWS), BF),
        pltpu.VMEM((2, HALF, 128), F32),
        pltpu.SemaphoreType.DMA((17,)),
    ]
    for first, width, route in PARTS:
        shape = second_shape(width)
        scratch += [
            pltpu.VMEM((4, BLOCK, width), BF),
            pltpu.VMEM((4, BLOCK, width), BF),
            pltpu.VMEM((2, 80, width), BF),
            pltpu.VMEM((2, BLOCK, width), BF),
            pltpu.VMEM((4,) + shape, BF),
            pltpu.VMEM((3,) + shape, BF),
            pltpu.VMEM((4, 16, width), BF),
            pltpu.VMEM((3, 16, width), BF),
        ]
    count = PER_PART * len(PARTS)
    scratch += [pltpu.SemaphoreType.DMA((count,)), pltpu.SemaphoreType.DMA((count,))]
    merged, final = pl.pallas_call(
        main_kernel,
        out_shape=(
            jax.ShapeDtypeStruct((ROWS // 4, 4 * D), BF),
            jax.ShapeDtypeStruct((16, COLS), F32),
        ),
        in_specs=[hbm] * 7,
        out_specs=(hbm, hbm),
        scratch_shapes=scratch,
        compiler_params=pltpu.CompilerParams(
            collective_id=0, has_side_effects=True, vmem_limit_bytes=62 * 2**20
        ),
        cost_estimate=pl.CostEstimate(
            flops=14_000_000_000, bytes_accessed=14_000_000, transcendentals=400_000
        ),
    )(window_live, window_index, merge_gain, patches, d_merged, w_qkv.T, w_out)
    merged, qkv, out, gain = pl.pallas_call(
        last_kernel,
        out_shape=(
            jax.ShapeDtypeStruct((ROWS // 4, 4 * D), BF),
            jax.ShapeDtypeStruct((SHARD, 3 * INNER), F32),
            jax.ShapeDtypeStruct((SHARD, INNER), F32),
            jax.ShapeDtypeStruct((1, SHARD), F32),
        ),
        in_specs=[vmem, vmem],
        out_specs=(vmem, vmem, vmem, vmem),
    )(final, merged)
    return merged, qkv, out.T, gain.reshape(SHARD)


def solution(mesh):
    both = ("dp", "vis")
    rows = P(both, None)
    return jax.shard_map(
        on_device,
        mesh=mesh,
        in_specs=(rows, rows, rows, rows, P(), P(), P()),
        out_specs=(rows, rows, P(None, both), P(both)),
        check_vma=False,
    )
```
